256 devices in a mesh: group: 4 (over z_hi, core), fsdp: 64 (over y, z_lo, x).
Axes of the slice: x: 4, y: 4, z: 8 (z_hi: 2, z_lo: 4; z = z_hi * 4 + z_lo), core: 2. Of those that a mesh axis runs over, the one named last changes fastest.
Arguments:
- tokens: bfloat16 [768, 8192], P(('group', 'fsdp')), may hold values from -6 to 6
- gate_master: bfloat16 [8192, 26624], P('group', 'fsdp'), may hold values from -0.4087961 to 0.4087961
- up_master: bfloat16 [8192, 26624], P('group', 'fsdp'), may hold values from -0.4087961 to 0.4087961
- hidden_cotangent: bfloat16 [768, 26624], P('group', 'fsdp'), may hold values from -1.75 to 1.75
Outputs:
- hidden: bfloat16 [768, 26624], P('group', 'fsdp')
- token_grad: bfloat16 [768, 8192], P(('group', 'fsdp'))
- gate_grad: bfloat16 [8192, 26624], P('group', 'fsdp')
- up_grad: bfloat16 [8192, 26624], P('group', 'fsdp')
The draws below stay inside these ranges and needn't reach their ends.
All inputs are finite; a program needn't handle non-finite values.
Results may differ from the reference program's by a relative error of at most 0.012.
Values may be sent and summed in bfloat16 or wider, within the bound.
A program may use at most 128 MiB of HBM per device.

```python
import math
import jax
import jax.numpy as jnp
from jax import lax

D = 8192
FF = 26624
TOKENS = 768
N_GROUP = 4
N_FSDP = 64


def master_copy(base, key, ramp):
    key_cols, key_rows = jax.random.split(key)
    position = jnp.arange(FF, dtype=jnp.float32) / FF
    columns = jnp.exp(jax.random.uniform(key_cols, (1, FF), jnp.float32, math.log(0.1), 0.0))
    columns = columns * (1.0 + ramp * position)[None, :]
    rows = jnp.exp(jax.random.uniform(key_rows, (D, 1), jnp.float32, 0.0, math.log(2.0)))
    return (base * columns * rows * D ** (-0.5)).astype(jnp.bfloat16)


def draw_gate_master(key, part):
    key = jax.random.fold_in(key, 11)
    key_base, key_scales = jax.random.split(key)
    base = jnp.clip(jax.random.normal(key_base, (D, FF), jnp.float32), -6.0, 6.0)
    return master_copy(base, key_scales, 2.0)


def draw_up_master(key, part):
    key = jax.random.fold_in(key, 23)
    key_base, key_scales = jax.random.split(key)
    base = jnp.clip(jax.random.normal(key_base, (D, FF), jnp.float32), -6.0, 6.0)
    return master_copy(base, key_scales, 2.0)


def spiked(entries, own_key, source, target, shards_of, factor):
    def block_of(dim):
        return (jnp.arange(entries.shape[dim]) // (entries.shape[dim] // shards_of)).reshape((-1,) + (1,) * (entries.ndim - 1 - dim))

    near = jax.random.permutation(own_key, shards_of)[block_of(target)]
    far = (block_of(target) + shards_of // 2) % shards_of
    return jnp.where((block_of(source) == near) | (block_of(source) == far), factor * entries, entries)


def shard_levels(key, shape, cuts, low, top_value):
    def one(dim, blocks):
        heights = jax.random.uniform(jax.random.fold_in(jax.random.fold_in(key, 6), dim), (blocks,), jnp.float32, low / len(cuts), top_value / len(cuts))
        return jnp.repeat(jnp.exp(heights), shape[dim] // blocks).reshape((-1,) + (1,) * (len(shape) - dim - 1))

    gain = one(*cuts[0])
    for cut in cuts[1:]:
        gain = gain * one(*cut)
    return gain


def centred(stream_key, extent, spread, limit, cuts=(), kind=jnp.bfloat16):
    entries = jax.random.normal(stream_key, extent, jnp.float32) * spread
    if len(cuts) > 0:
        entries = shard_levels(stream_key, extent, cuts, -0.22, 0.18) * entries
    return jnp.clip(entries, min=-limit, max=limit).astype(kind)


def heavy_noise(rng, dims, scale, most, pieces, heavy, held_as=jnp.bfloat16):
    drawn = scale * jax.random.normal(rng, dims, jnp.float32)
    if pieces:
        drawn = drawn * shard_levels(rng, dims, pieces, -0.22, 0.18)
    return jnp.clip(spiked(drawn, jax.random.fold_in(rng, 3), *heavy), -most, most).astype(held_as)


def setup_inputs(seed: int = 0) -> dict:
    key_list = jax.random.split(jax.random.key(seed), 5)
    return {
        "tokens": centred(key_list[0], (TOKENS, D), 1.0, 6.0, ((0, 256),)),
        "gate_master": draw_gate_master(jax.random.fold_in(key_list[4], 71), 0),
        "up_master": draw_up_master(jax.random.fold_in(key_list[4], 71), 0),
        "hidden_cotangent": heavy_noise(key_list[3], (TOKENS, FF), (3.0 / TOKENS ** 0.5), 1.75, ((0, 4), (1, 64)), (1, 0, 64, 4.0)),
    }


QMAX = 60.0
EPS = 1e-6


def quantize(master, amax):
    factor = QMAX / (amax + EPS)
    scaled = master.astype(jnp.float32) * factor
    return jnp.floor(scaled + 0.5).astype(jnp.bfloat16)


def reference(tokens, gate_master, up_master, hidden_cotangent):
    gate_amax = jnp.max(jnp.abs(gate_master)).astype(jnp.float32)
    up_amax = jnp.max(jnp.abs(up_master)).astype(jnp.float32)
    gate_scale = (gate_amax + EPS) / QMAX
    up_scale = (up_amax + EPS) / QMAX
    width = FF // N_FSDP
    count = tokens.shape[0]
    grouped = tokens.astype(jnp.float32).reshape(N_GROUP, count // N_GROUP, D)

    def block(token_grad, index):
        start = (index * width).astype(jnp.int32)
        gate_quant = quantize(lax.dynamic_slice_in_dim(gate_master, start, width, 1), gate_amax)
        up_quant = quantize(lax.dynamic_slice_in_dim(up_master, start, width, 1), up_amax)
        cotangent = lax.dynamic_slice_in_dim(hidden_cotangent, start, width, 1).astype(jnp.float32)
        gate = jnp.dot(tokens, gate_quant, preferred_element_type=jnp.float32) * gate_scale
        up = jnp.dot(tokens, up_quant, preferred_element_type=jnp.float32) * up_scale
        sig = jax.nn.sigmoid(gate)
        silu = gate * sig
        hidden = (silu * up).astype(jnp.bfloat16)
        gate_act = (cotangent * up * sig * (1.0 + gate * (1.0 - sig))).astype(jnp.bfloat16)
        up_act = (cotangent * silu).astype(jnp.bfloat16)
        token_grad = token_grad + jnp.dot(gate_act, gate_quant.T, preferred_element_type=jnp.float32) * gate_scale
        token_grad = token_grad + jnp.dot(up_act, up_quant.T, preferred_element_type=jnp.float32) * up_scale
        gate_part = jnp.einsum("gtd,gtf->gdf", grouped, gate_act.astype(jnp.float32).reshape(N_GROUP, -1, width))
        up_part = jnp.einsum("gtd,gtf->gdf", grouped, up_act.astype(jnp.float32).reshape(N_GROUP, -1, width))
        gate_grad = jnp.sum(lax.optimization_barrier(gate_part.astype(jnp.bfloat16)).astype(jnp.float32), axis=0).astype(jnp.bfloat16)
        up_grad = jnp.sum(lax.optimization_barrier(up_part.astype(jnp.bfloat16)).astype(jnp.float32), axis=0).astype(jnp.bfloat16)
        return token_grad, (hidden, gate_grad, up_grad)

    start_grad = jnp.zeros((count, D), jnp.float32)
    token_grad, stacked = lax.scan(block, start_grad, jnp.arange(N_FSDP, dtype=jnp.int32))
    hidden = jnp.moveaxis(stacked[0], 0, 1).reshape(count, FF)
    gate_grad = jnp.moveaxis(stacked[1], 0, 1).reshape(D, FF)
    up_grad = jnp.moveaxis(stacked[2], 0, 1).reshape(D, FF)
    return hidden, token_grad.astype(jnp.bfloat16), gate_grad, up_grad
```

```python
import functools

import jax
import jax.numpy as jnp
from jax import lax
from jax.experimental import pallas as pl
from jax.experimental.pallas import tpu as pltpu
from jax.sharding import PartitionSpec as P

QMAX = 60.0
EPS = 1e-06
MESH = pl.DeviceIdType.MESH
F32 = jnp.float32
BF16 = jnp.bfloat16

DQ = 2048
FW = 416
FA = 384
FT = FW - FA
FP = 896
ORDER = (1, 3, 2)


def position():
    g = lax.axis_index("group")
    f = lax.axis_index("fsdp")
    return lax.div(g, 2), lax.rem(g, 2), lax.div(f, 16), lax.rem(lax.div(f, 4), 4), lax.rem(f, 4)


def place(zh, c, y, zl, x):
    return {"group": zh * 2 + c, "fsdp": y * 16 + zl * 4 + x}


def absolute_row(s, w, y, x):
    d, ab = lax.div(s, 2), lax.rem(s, 2)
    r, u = lax.div(w, 8), lax.rem(w, 8)
    near, zls = lax.div(u, 2), lax.rem(u, 2)
    far_y, near_x = lax.rem(y + d, 4), lax.rem(x + near, 4)
    far_x, near_y = lax.rem(x + d, 4), lax.rem(y + near, 4)
    row_a = far_y * 16 + zls * 4 + near_x
    row_b = near_y * 16 + (zls + 2) * 4 + far_x
    return jnp.where(ab == 0, row_a, row_b) * 3 + r


def kernel(
    tokens, gate_hbm, up_hbm, cot,
    hidden_out, token_out, gate_out, up_out,
    S, tokb, scr, X, Wp, gm, um, am_tx, am_rx, cotp, cotr, cotf,
    Pf, Ps, Pr, Q, Qs, Qr, Ac, Asc, H, TS, TO, RT, R1s, R1r, R2f, R2s, R2r, R3s, R3r, tscr,
    GG, UG,
    load_sem, out_sem, tx, rx,
):
    zh, c, y, zl, x = position()
    sib = place(zh, 1 - c, y, zl, x)
    anti = place(1 - zh, c, y, zl, x)
    antisib = place(1 - zh, 1 - c, y, zl, x)
    group_peers = (sib, anti, antisib)

    def at_x(d):
        return place(zh, c, y, zl, lax.rem(x + d, 4))

    def at_y(d):
        return place(zh, c, lax.rem(y + d, 4), zl, x)

    def at_z(d):
        return place(zh, c, y, lax.rem(zl + d, 4), x)

    used = [0]
    copies = []

    def send(src, dst, to):
        i = used[0]
        used[0] += 1
        cp = pltpu.make_async_remote_copy(
            src_ref=src, dst_ref=dst, send_sem=tx.at[i], recv_sem=rx.at[i],
            device_id=to, device_id_type=MESH,
        )
        cp.start()
        copies.append(cp)
        return cp

    loads = []
    for i in range(4):
        rows = pl.ds(i * 512, 512)
        for k, (src, dst) in enumerate(((gate_hbm, gm), (up_hbm, um))):
            cp = pltpu.make_async_copy(src.at[rows], dst.at[rows], load_sem.at[i, k])
            cp.start()
            loads.append(cp)
    barrier = pltpu.get_barrier_semaphore()
    peers = list(group_peers)
    for d in (1, 2, 3):
        peers += [at_x(d), at_y(d), at_z(d)]
    for p in peers:
        pl.semaphore_signal(barrier, inc=1, device_id=p, device_id_type=MESH)

    for j in range(64):
        tscr[pl.ds(j, 3, stride=64), :] = tokens[:, j * 128:(j + 1) * 128].astype(F32)
    for g in range(4):
        for r in range(3):
            tokb[g, r] = tscr[pl.ds(r * 64 + g * 16, 16), :].astype(BF16)

    q = lax.broadcasted_iota(jnp.int32, (192, 192), 0)
    col = lax.broadcasted_iota(jnp.int32, (192, 192), 1)
    pick = (col == absolute_row(lax.div(q, 24), lax.rem(q, 24), y, x)).astype(F32).astype(BF16)
    cperm = jnp.dot(pick, cot[...], preferred_element_type=F32)
    cotf[zh] = cperm
    cotp[...] = cperm.astype(BF16)

    tops = [jnp.zeros((8, FW), F32), jnp.zeros((8, FW), F32)]
    for i in range(4):
        for k, ref in enumerate((gm, um)):
            loads[2 * i + k].wait()

            def largest(b, top, ref=ref, i=i):
                v = jnp.abs(ref[pl.ds(i * 512 + b * 64, 64), :].astype(F32))
                return jnp.maximum(top, jnp.max(v.reshape(8, 8, FW), axis=0))

            tops[k] = lax.fori_loop(0, 8, largest, tops[k])
    for k in range(2):
        am_tx[0, pl.ds(8 * k, 8), :] = jnp.broadcast_to(
            jnp.max(tops[k], axis=(0, 1), keepdims=True), (8, 128)
        )

    pl.semaphore_wait(barrier, len(peers))

    gi = c * 2 + zh
    near = S.at[lax.div(zl, 2), 0, lax.rem(zl, 2)]
    s0 = []
    for p, (pz, pc) in zip(group_peers, ((zh, 1 - c), (1 - zh, c), (1 - zh, 1 - c))):
        s0.append(send(tokb.at[pz * 2 + pc], near.at[gi], p))
    near[gi] = tokb[zh * 2 + c]

    def share(stage, to):
        return [send(am_tx.at[stage], am_rx.at[3 * stage + i], p) for i, p in enumerate(to)]

    def merge(stage, cps):
        v = am_tx[stage]
        for i, cp in enumerate(cps):
            cp.wait_recv()
            v = jnp.maximum(v, am_rx[3 * stage + i])
        am_tx[stage + 1] = v

    m0 = share(0, group_peers)
    for cp in s0:
        cp.wait_recv()
    s1 = [send(near, near, at_z(d)) for d in (1, 2, 3)]
    merge(0, m0)
    m1 = share(1, [at_x(d) for d in (1, 2, 3)])
    merge(1, m1)
    m2 = share(2, [at_y(d) for d in (1, 2, 3)])
    for cp in s1:
        cp.wait_recv()
    s2 = [[], []]
    for d in (1, 3, 2):
        s2[0].append(send(S.at[0, 0], S.at[0, d], at_x(4 - d)))
        s2[1].append(send(S.at[1, 0], S.at[1, d], at_y(4 - d)))
    merge(2, m2)
    m3 = share(3, [at_z(d) for d in (1, 2, 3)])
    merge(3, m3)
    cot_copy = send(cotp, cotr, anti)

    g_amax = jnp.max(am_tx[4, 0:8, :], axis=(0, 1), keepdims=True)
    u_amax = jnp.max(am_tx[4, 8:16, :], axis=(0, 1), keepdims=True)
    g_factor, u_factor = QMAX / (g_amax + EPS), QMAX / (u_amax + EPS)
    g_scale, u_scale = (g_amax + EPS) / QMAX, (u_amax + EPS) / QMAX

    @pl.loop(0, 32)
    def _(b):
        rows = pl.ds(pl.multiple_of(b * 64, 64), 64)
        wg = jnp.floor(gm[rows, :].astype(F32) * g_factor + 0.5)
        wu = jnp.floor(um[rows, :].astype(F32) * u_factor + 0.5)
        Wp[rows, 0:FA] = wg[:, :FA].astype(BF16)
        Wp[rows, FA:2 * FA] = wu[:, :FA].astype(BF16)
        tail = jnp.concatenate([wg[:, FA:], wu[:, FA:], jnp.zeros((64, 64), F32)], axis=1)
        Wp[rows, 2 * FA:FP] = tail.astype(BF16)

    big = {1: [], 2: [], 3: []}

    def far(ab):
        return at_y if ab == 0 else at_x

    for ab in range(2):
        for cp in s2[ab]:
            cp.wait_recv()
        scr[ab] = S[ab].reshape(1536, 128).astype(F32)
        for k in range(0, 12, 2):
            for fb in range(16):
                lo = scr[ab, pl.ds(k * 16 + fb, 8, stride=192), :]
                hi = scr[ab, pl.ds((k + 1) * 16 + fb, 8, stride=192), :]
                X[ab, 8 * k:8 * k + 16, fb * 128:(fb + 1) * 128] = jnp.concatenate(
                    [lo, hi], axis=0
                ).astype(BF16)
        for d in ORDER:
            big[d].append(send(X.at[ab], X.at[2 * d + ab], far(ab)(4 - d)))

    p_copies, q_copies, a_copies = {}, {}, {}

    def forward(d):
        xs = X[2 * d:2 * d + 2].reshape(192, DQ)
        for n in range(0, FP, 256):
            width = min(256, FP - n)
            part = jnp.dot(xs, Wp[:, n:n + width], preferred_element_type=F32)
            Pf[d, :, :, n:n + width] = part.reshape(4, 48, width)
        for ab in range(2):
            Ps[d, ab] = Pf[d, 2 * ab + 1 - c].astype(BF16)
            p_copies[d, ab] = send(Ps.at[d, ab], Pr.at[d, ab], sib)

    def chip_sum(d, ab):
        p_copies[d, ab].wait_recv()
        v = Pf[d, 2 * ab + c] + Pr[d, ab].astype(F32)
        Q[d, ab] = v
        Qs[d, ab] = v.astype(BF16)

    def cross(d, ab):
        q_copies[d, ab] = send(Qs.at[d, ab], Qr.at[d, ab], anti)

    def act(d, ab):
        q_copies[d, ab].wait_recv()
        s = 2 * d + ab
        pre = Q[d, ab] + Qr[d, ab].astype(F32)
        gate = jnp.concatenate([pre[:, :FA], pre[:, 2 * FA:2 * FA + FT]], axis=1) * g_scale
        up = jnp.concatenate([pre[:, FA:2 * FA], pre[:, 2 * FA + FT:2 * FA + 2 * FT]], axis=1) * u_scale
        cotangent = cotf[:, s * 24:s * 24 + 24, :].reshape(48, FW)
        sig = jax.nn.sigmoid(gate)
        silu = gate * sig
        H[s * 48:s * 48 + 48, :] = (silu * up).astype(BF16)
        ga = cotangent * up * sig * (1.0 + gate * (1.0 - sig))
        ua = cotangent * silu
        packed = jnp.concatenate(
            [ga[:, :FA], ua[:, :FA], ga[:, FA:], ua[:, FA:], jnp.zeros((48, 64), F32)], axis=1
        )
        Ac[s, c] = packed.astype(BF16)
        a_copies[d, ab] = send(Ac.at[s, c], Ac.at[s, c], sib)

    lane = lax.broadcasted_iota(jnp.int32, (1, FP), 1)
    is_gate = (lane < FA) | ((lane >= 2 * FA) & (lane < 2 * FA + FT))
    scale_row = jnp.where(is_gate, g_scale, u_scale)

    def backward(d):
        for ab in range(2):
            a_copies[d, ab].wait_recv()
        Asc[...] = (Ac[2 * d:2 * d + 2].reshape(192, FP).astype(F32) * scale_row).astype(BF16)

        @pl.loop(0, 8)
        def _(j):
            cols = pl.ds(pl.multiple_of(j * 256, 256), 256)
            part = lax.dot_general(
                Asc[...], Wp[cols, :], (((1,), (1,)), ((), ())), preferred_element_type=F32
            )
            if d == 0:
                TO[:, cols] = part
            else:
                TS[d - 1, :, cols] = part.astype(BF16)

    rs = [[], []]

    def scatter(d):
        for ab in range(2):
            rs[ab].append(send(TS.at[d - 1, pl.ds(ab * 96, 96)], RT.at[d - 1, ab], far(ab)(d)))

    forward(0)
    chip_sum(0, 0)
    cross(0, 0)
    chip_sum(0, 1)
    for i, d in enumerate(ORDER):
        for cp in big[d]:
            cp.wait_recv()
        forward(d)
        for ab in range(2):
            chip_sum(d, ab)
            cross(d, ab)
        if i == 1:
            cot_copy.wait_recv()
            cotf[1 - zh] = cotr[...].astype(F32)
            act(0, 0)
    cross(0, 1)
    for d in ORDER:
        for ab in range(2):
            act(d, ab)
        backward(d)
        scatter(d)
    act(0, 1)
    backward(0)

    row = lax.broadcasted_iota(jnp.int32, (192, 384), 0)
    q = lax.broadcasted_iota(jnp.int32, (192, 384), 1)
    s, w = lax.div(q, 48), lax.rem(q, 48)
    mine = lax.div(w, 24) == zh
    pick = (mine & (row == absolute_row(s, lax.rem(w, 24), y, x))).astype(F32).astype(BF16)
    hidden_out[...] = jnp.dot(pick, H[...], preferred_element_type=F32).astype(BF16)

    def weight_grads(first, last):
        @pl.loop(first, last)
        def _(j):
            rows = pl.ds(pl.multiple_of(j * 256, 256), 256)
            part = lax.dot_general(
                X[:, :, rows].reshape(768, 256), Ac[...].reshape(768, FP),
                (((0,), (0,)), ((), ())), preferred_element_type=F32,
            )
            GG[rows, :] = jnp.concatenate(
                [part[:, :FA], part[:, 2 * FA:2 * FA + FT]], axis=1
            ).astype(BF16)
            UG[rows, :] = jnp.concatenate(
                [part[:, FA:2 * FA], part[:, 2 * FA + FT:2 * FA + 2 * FT]], axis=1
            ).astype(BF16)
            pltpu.make_async_copy(GG.at[rows], gate_out.at[rows], out_sem.at[j, 0]).start()
            pltpu.make_async_copy(UG.at[rows], up_out.at[rows], out_sem.at[j, 1]).start()

    weight_grads(0, 2)

    r1 = [[], []]
    for ab in range(2):
        for cp in rs[ab]:
            cp.wait_recv()
        for fb in range(16):
            cols = slice(fb * 128, (fb + 1) * 128)
            v = TO[ab * 96:ab * 96 + 96, cols]
            for i in range(3):
                v = v + RT[i, ab, :, cols].astype(F32)
            for k in range(12):
                scr[ab, pl.ds(k * 16 + fb, 8, stride=192), :] = v[8 * k:8 * k + 8]
        R1s[ab] = scr[ab].astype(BF16).reshape(4, 2, 4, 3, 16, 128)
        near_at = at_x if ab == 0 else at_y
        for d in (1, 3, 2):
            r1[ab].append(send(R1s.at[ab, d], R1r.at[ab, d - 1], near_at(d)))
    weight_grads(2, 4)
    for ab in range(2):
        for cp in r1[ab]:
            cp.wait_recv()
        v = scr[ab, 0:384, :]
        for i in range(3):
            v = v + R1r[ab, i].reshape(384, 128).astype(F32)
        R2f[2 * ab:2 * ab + 2] = v.reshape(2, 192, 128)
        R2s[2 * ab:2 * ab + 2] = v.astype(BF16).reshape(2, 4, 3, 16, 128)
    r2 = [send(R2s.at[lax.rem(zl + d, 4)], R2r.at[d - 1], at_z(d)) for d in (1, 2, 3)]
    weight_grads(4, 6)
    v = R2f[zl]
    for i, cp in enumerate(r2):
        cp.wait_recv()
        v = v + R2r[i].reshape(192, 128).astype(F32)
    R2f[zl] = v
    R3s[...] = v.astype(BF16).reshape(4, 3, 16, 128)
    r3 = []
    for i, (pz, pc) in enumerate(((zh, 1 - c), (1 - zh, c), (1 - zh, 1 - c))):
        r3.append(send(R3s.at[pc * 2 + pz], R3r.at[i], group_peers[i]))
    weight_grads(6, 8)
    for r in range(3):
        at = pl.ds(pl.multiple_of(r * 64 + (zh * 2 + c) * 16, 16), 16)
        tscr[at, :] = R2f[zl, pl.ds(pl.multiple_of(gi * 48 + r * 16, 16), 16), :]
    for i, (pz, pc) in enumerate(((zh, 1 - c), (1 - zh, c), (1 - zh, 1 - c))):
        r3[i].wait_recv()
        for r in range(3):
            at = pl.ds(pl.multiple_of(r * 64 + (pz * 2 + pc) * 16, 16), 16)
            tscr[at, :] = R3r[i, r].astype(F32)
    for j in range(64):
        token_out[:, j * 128:(j + 1) * 128] = tscr[pl.ds(j, 3, stride=64), :].astype(BF16)

    for cp in copies:
        cp.wait_send()

    @pl.loop(0, 8)
    def _(j):
        rows = pl.ds(pl.multiple_of(j * 256, 256), 256)
        pltpu.make_async_copy(GG.at[rows], gate_out.at[rows], out_sem.at[j, 0]).wait()
        pltpu.make_async_copy(UG.at[rows], up_out.at[rows], out_sem.at[j, 1]).wait()


def on_device(tokens, gate_master, up_master, hidden_cotangent):
    vmem = pl.BlockSpec(memory_space=pltpu.VMEM)
    anywhere = pl.BlockSpec(memory_space=pl.ANY)
    V = pltpu.VMEM
    n_copies = 96
    return pl.pallas_call(
        kernel,
        out_shape=(
            jax.ShapeDtypeStruct((192, FW), BF16),
            jax.ShapeDtypeStruct((3, 8192), BF16),
            jax.ShapeDtypeStruct((DQ, FW), BF16),
            jax.ShapeDtypeStruct((DQ, FW), BF16),
        ),
        in_specs=[vmem, anywhere, anywhere, vmem],
        out_specs=(vmem, vmem, anywhere, anywhere),
        scratch_shapes=[
            V((2, 4, 2, 4, 3, 16, 128), BF16),
            V((4, 3, 16, 128), BF16),
            V((2, 1536, 128), F32),
            V((8, 96, DQ), BF16),
            V((DQ, FP), BF16),
            V((DQ, FW), BF16),
            V((DQ, FW), BF16),
            V((5, 16, 128), F32),
            V((12, 16, 128), F32),
            V((192, FW), BF16),
            V((192, FW), BF16),
            V((2, 192, FW), F32),
            V((4, 4, 48, FP), F32),
            V((4, 2, 48, FP), BF16),
            V((4, 2, 48, FP), BF16),
            V((4, 2, 48, FP), F32),
            V((4, 2, 48, FP), BF16),
            V((4, 2, 48, FP), BF16),
            V((8, 2, 48, FP), BF16),
            V((192, FP), BF16),
            V((384, FW), BF16),
            V((3, 192, DQ), BF16),
            V((192, DQ), F32),
            V((3, 2, 96, DQ), BF16),
            V((2, 4, 2, 4, 3, 16, 128), BF16),
            V((2, 3, 2, 4, 3, 16, 128), BF16),
            V((4, 192, 128), F32),
            V((4, 4, 3, 16, 128), BF16),
            V((3, 4, 3, 16, 128), BF16),
            V((4, 3, 16, 128), BF16),
            V((3, 3, 16, 128), BF16),
            V((192, 128), F32),
            V((DQ, FW), BF16),
            V((DQ, FW), BF16),
            pltpu.SemaphoreType.DMA((4, 2)),
            pltpu.SemaphoreType.DMA((8, 2)),
            pltpu.SemaphoreType.DMA((n_copies,)),
            pltpu.SemaphoreType.DMA((n_copies,)),
        ],
        compiler_params=pltpu.CompilerParams(
            collective_id=0, has_side_effects=True, vmem_limit_bytes=58 * 2**20
        ),
        name="swiglu_step",
    )(tokens, gate_master, up_master, hidden_cotangent)


def solution(mesh):
    placed = (
        P(("group", "fsdp"), None),
        P("group", "fsdp"),
        P("group", "fsdp"),
        P("group", "fsdp"),
    )
    return jax.shard_map(
        on_device,
        mesh=mesh,
        in_specs=placed,
        out_specs=(
            P("group", "fsdp"),
            P(("group", "fsdp"), None),
            P("group", "fsdp"),
            P("group", "fsdp"),
        ),
        check_vma=False,
    )
```

```python
import functools

import jax
import jax.numpy as jnp
from jax import lax
from jax.experimental import pallas as pl
from jax.experimental.pallas import tpu as pltpu
from jax.sharding import PartitionSpec as P

QMAX = 60.0
EPS = 1e-06
MESH = pl.DeviceIdType.MESH
F32 = jnp.float32
BF16 = jnp.bfloat16

DQ = 2048
FW = 416
FA = 384
FT = FW - FA
FP = 2 * FW
SEAT = tuple((k % 2) * 6 + (k // 2 % 2) * 3 + k // 4 for k in range(12))
LOADS = ((0, 112), (112, 112), (224, 96), (320, 96))
FAR = (1, 3, 2)


def position():
    g = lax.axis_index("group")
    f = lax.axis_index("fsdp")
    return lax.div(g, 2), lax.rem(g, 2), lax.div(f, 16), lax.rem(lax.div(f, 4), 4), lax.rem(f, 4)


def place(zh, c, y, zl, x):
    return {"group": zh * 2 + c, "fsdp": y * 16 + zl * 4 + x}


def absolute_row(n, y, x):
    chunk, i, u = lax.div(n, 48), lax.div(lax.rem(n, 48), 8), lax.rem(n, 8)
    ab, three = lax.div(i, 3), lax.rem(i, 3)
    near, zls = lax.div(u, 2), lax.rem(u, 2)
    d = jnp.where(chunk == 0, 0, jnp.where(three == 0, FAR[0], jnp.where(three == 1, FAR[1], FAR[2])))
    r = jnp.where(chunk == 0, three, chunk - 1)
    row_a = lax.rem(y + d, 4) * 16 + zls * 4 + lax.rem(x + near, 4)
    row_b = lax.rem(y + near, 4) * 16 + (zls + 2) * 4 + lax.rem(x + d, 4)
    return jnp.where(ab == 0, row_a, row_b) * 3 + r


def kernel(
    tokens, gate_hbm, up_hbm, cot,
    hidden_out, token_out, gate_out, up_out,
    S, tokb, TK, scr, X, Wt, gm, um, am_tx, am_rx, cotf,
    Pf, Ps, Pr, Qs, Qr, Ag, Ax, Asc, H, TS, TO, RT, scr2, R1s, R1r, R2f, R2s, R2r, acc, R3s, R3r, R3f, tscr,
    At, GG, UG,
    load_sem, out_sem, tx, rx,
):
    zh, c, y, zl, x = position()
    sib = place(zh, 1 - c, y, zl, x)
    anti = place(1 - zh, c, y, zl, x)
    z = zh * 4 + zl

    def at_x(d):
        return place(zh, c, y, zl, lax.rem(x + d, 4))

    def at_y(d):
        return place(zh, c, lax.rem(y + d, 4), zl, x)

    def at_z(d):
        to = lax.rem(z + d, 8)
        return place(lax.div(to, 4), c, y, lax.rem(to, 4), x)

    xs_to, ys_to = [at_x(d) for d in (1, 2, 3)], [at_y(d) for d in (1, 2, 3)]
    zs_to = [at_z(d) for d in range(1, 8)]

    used = [0]
    copies = []

    def send(src, dst, to):
        i = used[0]
        used[0] += 1
        cp = pltpu.make_async_remote_copy(
            src_ref=src, dst_ref=dst, send_sem=tx.at[i], recv_sem=rx.at[i],
            device_id=to, device_id_type=MESH,
        )
        cp.start()
        copies.append(cp)
        return cp

    loads = []
    for i, (start, count) in enumerate(LOADS):
        rows = pl.ds(start, count)
        for k, (src, dst) in enumerate(((gate_hbm, gm), (up_hbm, um))):
            cp = pltpu.make_async_copy(src.at[rows], dst.at[rows], load_sem.at[i, k])
            cp.start()
            loads.append(cp)
    barrier = pltpu.get_barrier_semaphore()
    peers = [sib] + xs_to + ys_to + zs_to
    for p in peers:
        pl.semaphore_signal(barrier, inc=1, device_id=p, device_id_type=MESH)

    for j in range(64):
        tscr[pl.ds(j, 3, stride=64), :] = tokens[:, j * 128:(j + 1) * 128].astype(F32)
    for g in range(4):
        for r in range(3):
            tokb[g % 2, g // 2, r] = tscr[pl.ds(r * 64 + g * 16, 16), :].astype(BF16)

    pl.semaphore_wait(barrier, len(peers))

    t0 = send(tokb.at[1 - c], TK.at[:, c], sib)
    TK[:, c] = tokb[c]

    tops = [jnp.zeros((16, DQ), BF16), jnp.zeros((16, DQ), BF16)]
    for i, (start, count) in enumerate(LOADS):
        for k, ref in enumerate((gm, um)):
            loads[2 * i + k].wait()

            def largest(b, top, ref=ref, start=start):
                rows = pl.ds(pl.multiple_of(start + b * 16, 16), 16)
                return jnp.maximum(top, jnp.abs(ref[rows, :]))

            tops[k] = lax.fori_loop(0, count // 16, largest, tops[k])
    for k in range(2):
        am_tx[0, pl.ds(8 * k, 8), :] = jnp.broadcast_to(
            jnp.max(tops[k].astype(F32), axis=(0, 1), keepdims=True), (8, 128)
        )

    def share(stage, first, to):
        return [send(am_tx.at[stage], am_rx.at[first + i], p) for i, p in enumerate(to)]

    def merge(stage, first, cps):
        v = am_tx[stage]
        for i, cp in enumerate(cps):
            cp.wait_recv()
            v = jnp.maximum(v, am_rx[first + i])
        am_tx[stage + 1] = v

    m = share(0, 0, [sib])
    t0.wait_recv()
    near = S.at[lax.div(zl, 2), 0, lax.rem(zl, 2), zh]
    t1 = []
    for d, p in enumerate(zs_to):
        t1.append(send(TK.at[lax.div(lax.rem(z + d + 1, 8), 4)], near, p))
    near[...] = TK[zh]
    merge(0, 0, m)
    m = share(1, 1, xs_to)

    mine = absolute_row(lax.broadcasted_iota(jnp.int32, (192, 1), 0), y, x)
    col = lax.broadcasted_iota(jnp.int32, (192, 192), 1)
    pick = (col == mine).astype(F32).astype(BF16)
    cotf[...] = jnp.dot(pick, cot[...], preferred_element_type=F32)
    merge(1, 1, m)
    m = share(2, 4, ys_to)
    merge(2, 4, m)
    m = share(3, 7, zs_to)
    for cp in t1:
        cp.wait_recv()
    s2 = [[], []]
    for d in (1, 3, 2):
        s2[0].append(send(S.at[0, 0], S.at[0, d], at_x(4 - d)))
        s2[1].append(send(S.at[1, 0], S.at[1, d], at_y(4 - d)))
    merge(3, 7, m)

    g_amax = jnp.max(am_tx[4, 0:8, :], axis=(0, 1), keepdims=True)
    u_amax = jnp.max(am_tx[4, 8:16, :], axis=(0, 1), keepdims=True)
    g_factor, u_factor = QMAX / (g_amax + EPS), QMAX / (u_amax + EPS)
    g_scale, u_scale = (g_amax + EPS) / QMAX, (u_amax + EPS) / QMAX

    def quantized(ref, rows, factor):
        return jnp.floor(ref[rows, :].astype(F32) * factor + 0.5).astype(BF16)

    @pl.loop(0, FA // 16)
    def _(b):
        rows = pl.ds(pl.multiple_of(b * 16, 16), 16)
        Wt[rows, :] = quantized(gm, rows, g_factor)
        Wt[pl.ds(pl.multiple_of(FA + b * 16, 16), 16), :] = quantized(um, rows, u_factor)

    for t in range(0, FT, 16):
        Wt[2 * FA + t:2 * FA + t + 16, :] = quantized(gm, pl.ds(FA + t, 16), g_factor)
        Wt[2 * FA + FT + t:2 * FA + FT + t + 16, :] = quantized(um, pl.ds(FA + t, 16), u_factor)

    def far(ab):
        return at_y if ab == 0 else at_x

    for ab in range(2):
        for cp in s2[ab]:
            cp.wait_recv()
        scr[ab] = S[ab].reshape(1536, 128).astype(F32)
        for k in range(0, 12, 2):
            for fb in range(16):
                lo = scr[ab, pl.ds(SEAT[k] * 16 + fb, 8, stride=192), :]
                hi = scr[ab, pl.ds(SEAT[k + 1] * 16 + fb, 8, stride=192), :]
                at = ab * 96 + 8 * k
                X[0, at:at + 16, fb * 128:(fb + 1) * 128] = jnp.concatenate([lo, hi], axis=0).astype(BF16)

    big = {}

    def gather(q):
        big[q] = []
        for t, d in enumerate(FAR):
            for ab in range(2):
                own = pl.ds(ab * 96 + (q - 1) * 32, 32)
                there = pl.ds((ab * 3 + t) * 32, 32)
                big[q].append(send(X.at[0, own], X.at[q, there], far(ab)(4 - d)))

    p_copies, q_copies, sib_copies, anti_copies, fwd_copies = {}, {}, {}, {}, {}

    def forward(q):
        for n in range(0, FP, 256):
            width = min(256, FP - n)
            part = lax.dot_general(
                X[q], Wt[n:n + width, :], (((1,), (1,)), ((), ())), preferred_element_type=F32
            )
            for i in range(6):
                for k in range(4):
                    at = (i * 4 + k) * 8
                    Pf[q, k // 2, k % 2, i * 8:i * 8 + 8, n:n + width] = part[at:at + 8]
        Ps[q] = Pf[q, 1 - c].astype(BF16)
        p_copies[q] = send(Ps.at[q], Pr.at[q], sib)

    def cross(q):
        p_copies[q].wait_recv()
        Qs[q] = (Pf[q, c, 1 - zh] + Pr[q, 1 - zh].astype(F32)).astype(BF16)
        q_copies[q] = send(Qs.at[q], Qr.at[q], anti)

    def act(q):
        own = Pf[q, c, zh] + Pr[q, zh].astype(F32)
        q_copies[q].wait_recv()
        pre = own + Qr[q].astype(F32)
        gate = jnp.concatenate([pre[:, :FA], pre[:, 2 * FA:2 * FA + FT]], axis=1) * g_scale
        up = jnp.concatenate([pre[:, FA:2 * FA], pre[:, 2 * FA + FT:FP]], axis=1) * u_scale
        cotangent = cotf[q * 48:q * 48 + 48, :]
        sig = jax.nn.sigmoid(gate)
        silu = gate * sig
        H[q * 48:q * 48 + 48, :] = (silu * up).astype(BF16)
        ga = cotangent * up * sig * (1.0 + gate * (1.0 - sig))
        ua = cotangent * silu
        packed = jnp.concatenate([ga[:, :FA], ua[:, :FA], ga[:, FA:], ua[:, FA:]], axis=1)
        Ag[q, c, zh] = packed.astype(BF16)
        sib_copies[q] = send(Ag.at[q, c, zh], Ag.at[q, c, zh], sib)

    def cross_back(q):
        anti_copies[q] = send(Ag.at[q, c, zh], Ag.at[q, c, zh], anti)

    def pass_on(q):
        anti_copies[q].wait_recv()
        fwd_copies[q] = send(Ag.at[q, c, 1 - zh], Ag.at[q, c, 1 - zh], sib)

    lane = lax.broadcasted_iota(jnp.int32, (1, FP), 1)
    is_gate = (lane < FA) | ((lane >= 2 * FA) & (lane < 2 * FA + FT))
    scale_row = jnp.where(is_gate, g_scale, u_scale)
    rs = {}

    def backward(q):
        sib_copies[q].wait_recv()
        fwd_copies[q].wait_recv()
        parts = [Ag[q, k // 2, k % 2].astype(F32) for k in range(4)]
        rows = jnp.concatenate(
            [parts[k][i * 8:i * 8 + 8] for i in range(6) for k in range(4)], axis=0
        )
        Ax[q] = rows.astype(BF16)
        Asc[...] = (rows * scale_row).astype(BF16)
        for f in range(2):

            @pl.loop(0, 4)
            def _(j):
                cols = pl.ds(pl.multiple_of(j * 256, 256), 256)
                from_ = pl.ds(pl.multiple_of(f * 1024 + j * 256, 256), 256)
                part = jnp.dot(Asc[...], Wt[:, from_], preferred_element_type=F32)
                if q == 0:
                    TO[f, :, cols] = part
                else:
                    TS[q - 1, f, :, cols] = part.astype(BF16)

            if q == 3:
                scatter(q, f)
        if q in (1, 2):
            scatter(q, None)

    def scatter(q, f):
        fs = slice(None) if f is None else f
        rs[q, f] = []
        for t, d in enumerate(FAR):
            for ab in range(2):
                here = pl.ds((ab * 3 + t) * 32, 32)
                there = pl.ds((q - 1) * 32, 32)
                rs[q, f].append(
                    send(TS.at[q - 1, fs, here], RT.at[fs, ab, d - 1, there], far(ab)(d))
                )

    gather(1)
    forward(0)
    gather(2)
    cross(0)
    for cp in big[1]:
        cp.wait_recv()
    forward(1)
    gather(3)
    cross(1)
    act(0)
    for cp in big[2]:
        cp.wait_recv()
    forward(2)
    cross(2)
    act(1)
    cross_back(1)
    for cp in big[3]:
        cp.wait_recv()
    forward(3)
    cross(3)
    act(2)
    cross_back(2)
    pass_on(1)
    backward(1)
    act(3)
    cross_back(3)
    cross_back(0)
    pass_on(2)
    backward(2)
    pass_on(3)
    backward(3)
    pass_on(0)
    backward(0)

    row = lax.broadcasted_iota(jnp.int32, (192, 192), 0)
    mine = absolute_row(lax.broadcasted_iota(jnp.int32, (1, 192), 1), y, x)
    pick = (row == mine).astype(F32).astype(BF16)
    hidden_out[...] = jnp.dot(pick, H[...], preferred_element_type=F32).astype(BF16)

    for i in range(6):
        At[:, i * 128:(i + 1) * 128] = Ax[...].reshape(768, FP)[i * 128:(i + 1) * 128, :].T

    def weight_grads(first, last):
        @pl.loop(first, last)
        def _(j):
            cols = pl.ds(pl.multiple_of(j * 256, 256), 256)
            part = jnp.dot(
                At[...], X[:, :, cols].reshape(768, 256), preferred_element_type=F32
            ).astype(BF16)
            GG[0:FA, cols] = part[0:FA]
            GG[FA:FW, cols] = part[2 * FA:2 * FA + FT]
            UG[0:FA, cols] = part[FA:2 * FA]
            UG[FA:FW, cols] = part[2 * FA + FT:FP]
            pltpu.make_async_copy(GG.at[:, cols], gate_out.at[:, cols], out_sem.at[j, 0]).start()
            pltpu.make_async_copy(UG.at[:, cols], up_out.at[:, cols], out_sem.at[j, 1]).start()

    weight_grads(0, 3)

    def near_scatter(f):
        out = [[], []]
        for cp in rs[3, f]:
            cp.wait_recv()
        for ab in range(2):
            for fb in range(8):
                cols = slice(fb * 128, (fb + 1) * 128)
                v = TO[f, ab * 96:ab * 96 + 96, cols]
                for i in range(3):
                    v = v + RT[f, ab, i, :, cols].astype(F32)
                for k in range(12):
                    scr2[f, ab, pl.ds(SEAT[k] * 8 + fb, 8, stride=96), :] = v[8 * k:8 * k + 8]
            R1s[f, ab] = scr2[f, ab].astype(BF16).reshape(4, 192, 128)
            near_at = at_x if ab == 0 else at_y
            for d in FAR:
                out[ab].append(send(R1s.at[f, ab, d], R1r.at[f, ab, d - 1], near_at(d)))
        return out

    def column_scatter(f, r1):
        for ab in range(2):
            for cp in r1[ab]:
                cp.wait_recv()
            v = scr2[f, ab, 0:192, :]
            for i in range(3):
                v = v + R1r[f, ab, i].astype(F32)
            R2f[f, 2 * ab:2 * ab + 2] = v.reshape(2, 2, 48, 128)
            R2s[f, 2 * ab:2 * ab + 2] = v.astype(BF16).reshape(2, 2, 48, 128)
        out = []
        for d, p in enumerate(zs_to):
            to = lax.rem(z + d + 1, 8)
            out.append(send(R2s.at[f, lax.rem(to, 4), lax.div(to, 4)], R2r.at[f, d], p))
        return out

    def column_sum(f, r2):
        acc[f, zh] = R2f[f, zl, zh]
        acc[f, 1 - zh] = jnp.zeros((48, 128), F32)
        for d, cp in enumerate(r2):
            cp.wait_recv()
            half = lax.div(lax.rem(z + 7 - d, 8), 4)
            acc[f, half] = acc[f, half] + R2r[f, d].astype(F32)

    for q in (1, 2):
        for cp in rs[q, None]:
            cp.wait_recv()
    r1a = near_scatter(0)
    r1b = near_scatter(1)
    weight_grads(3, 4)
    r2a = column_scatter(0, r1a)
    r2b = column_scatter(1, r1b)
    weight_grads(4, 7)
    column_sum(0, r2a)
    column_sum(1, r2b)
    theirs = pl.ds(pl.multiple_of((1 - c) * 24, 8), 24)
    R3s[...] = jnp.concatenate(
        [acc[f, h, theirs, :] for h in range(2) for f in range(2)], axis=0
    ).astype(BF16)
    r3 = send(R3s, R3r, sib)
    weight_grads(7, 8)
    for h in range(2):
        for f in range(2):
            for r in range(3):
                at = pl.ds(pl.multiple_of(r * 64 + (h * 2 + c) * 16 + f * 8, 8), 8)
                tscr[at, :] = acc[f, h, pl.ds(pl.multiple_of(c * 24 + r * 8, 8), 8), :]
    r3.wait_recv()
    R3f[...] = R3r[...].astype(F32)
    for h in range(2):
        for f in range(2):
            for r in range(3):
                at = pl.ds(pl.multiple_of(r * 64 + (h * 2 + 1 - c) * 16 + f * 8, 8), 8)
                b = (h * 2 + f) * 24 + r * 8
                tscr[at, :] = R3f[b:b + 8, :]
    for j in range(64):
        token_out[:, j * 128:(j + 1) * 128] = tscr[pl.ds(j, 3, stride=64), :].astype(BF16)

    for cp in copies:
        cp.wait_send()

    @pl.loop(0, 8)
    def _(j):
        cols = pl.ds(pl.multiple_of(j * 256, 256), 256)
        pltpu.make_async_copy(GG.at[:, cols], gate_out.at[:, cols], out_sem.at[j, 0]).wait()
        pltpu.make_async_copy(UG.at[:, cols], up_out.at[:, cols], out_sem.at[j, 1]).wait()


def on_device(tokens, gate_master, up_master, hidden_cotangent):
    vmem = pl.BlockSpec(memory_space=pltpu.VMEM)
    anywhere = pl.BlockSpec(memory_space=pl.ANY)
    V = pltpu.VMEM
    n_copies = 128
    hidden, token_grad, gate_grad, up_grad = pl.pallas_call(
        kernel,
        out_shape=(
            jax.ShapeDtypeStruct((192, FW), BF16),
            jax.ShapeDtypeStruct((3, 8192), BF16),
            jax.ShapeDtypeStruct((FW, DQ), BF16),
            jax.ShapeDtypeStruct((FW, DQ), BF16),
        ),
        in_specs=[vmem, anywhere, anywhere, vmem],
        out_specs=(vmem, vmem, anywhere, anywhere),
        scratch_shapes=[
            V((2, 4, 2, 2, 2, 3, 16, 128), BF16),
            V((2, 2, 3, 16, 128), BF16),
            V((2, 2, 3, 16, 128), BF16),
            V((2, 1536, 128), F32),
            V((4, 192, DQ), BF16),
            V((FP, DQ), BF16),
            V((FW, DQ), BF16),
            V((FW, DQ), BF16),
            V((5, 16, 128), F32),
            V((14, 16, 128), F32),
            V((192, FW), F32),
            V((4, 2, 2, 48, FP), F32),
            V((4, 2, 48, FP), BF16),
            V((4, 2, 48, FP), BF16),
            V((4, 48, FP), BF16),
            V((4, 48, FP), BF16),
            V((4, 2, 2, 48, FP), BF16),
            V((4, 192, FP), BF16),
            V((192, FP), BF16),
            V((192, FW), BF16),
            V((3, 2, 192, 1024), BF16),
            V((2, 192, 1024), F32),
            V((2, 2, 3, 96, 1024), BF16),
            V((2, 2, 768, 128), F32),
            V((2, 2, 4, 192, 128), BF16),
            V((2, 2, 3, 192, 128), BF16),
            V((2, 4, 2, 48, 128), F32),
            V((2, 4, 2, 48, 128), BF16),
            V((2, 7, 48, 128), BF16),
            V((2, 2, 48, 128), F32),
            V((96, 128), BF16),
            V((96, 128), BF16),
            V((96, 128), F32),
            V((192, 128), F32),
            V((FP, 768), BF16),
            V((FW, DQ), BF16),
            V((FW, DQ), BF16),
            pltpu.SemaphoreType.DMA((4, 2)),
            pltpu.SemaphoreType.DMA((8, 2)),
            pltpu.SemaphoreType.DMA((n_copies,)),
            pltpu.SemaphoreType.DMA((n_copies,)),
        ],
        compiler_params=pltpu.CompilerParams(
            collective_id=0, has_side_effects=True, vmem_limit_bytes=58 * 2**20
        ),
        name="swiglu_step",
    )(tokens, gate_master.T, up_master.T, hidden_cotangent)
    return hidden, token_grad, gate_grad.T, up_grad.T


def solution(mesh):
    placed = (
        P(("group", "fsdp"), None),
        P("group", "fsdp"),
        P("group", "fsdp"),
        P("group", "fsdp"),
    )
    return jax.shard_map(
        on_device,
        mesh=mesh,
        in_specs=placed,
        out_specs=(
            P("group", "fsdp"),
            P(("group", "fsdp"), None),
            P("group", "fsdp"),
            P("group", "fsdp"),
        ),
        check_vma=False,
    )
```

```python
import functools

import jax
import jax.numpy as jnp
from jax import lax
from jax.experimental import pallas as pl
from jax.experimental.pallas import tpu as pltpu
from jax.sharding import PartitionSpec as P

QMAX = 60.0
EPS = 1e-06
MESH = pl.DeviceIdType.MESH
F32 = jnp.float32
BF16 = jnp.bfloat16

DQ = 2048
FW = 416
FA = 384
FT = FW - FA
FP = 2 * FW
SEAT = tuple((k % 2) * 6 + (k // 2 % 2) * 3 + k // 4 for k in range(12))
LOADS = ((0, 112), (112, 112), (224, 96), (320, 96))
FAR = (1, 3, 2)


def position():
    g = lax.axis_index("group")
    f = lax.axis_index("fsdp")
    return lax.div(g, 2), lax.rem(g, 2), lax.div(f, 16), lax.rem(lax.div(f, 4), 4), lax.rem(f, 4)


def place(zh, c, y, zl, x):
    return {"group": zh * 2 + c, "fsdp": y * 16 + zl * 4 + x}


def absolute_row(n, y, x):
    chunk, i, u = lax.div(n, 48), lax.div(lax.rem(n, 48), 8), lax.rem(n, 8)
    ab, three = lax.div(i, 3), lax.rem(i, 3)
    near, zls = lax.div(u, 2), lax.rem(u, 2)
    d = jnp.where(chunk == 0, 0, jnp.where(three == 0, FAR[0], jnp.where(three == 1, FAR[1], FAR[2])))
    r = jnp.where(chunk == 0, three, chunk - 1)
    row_a = lax.rem(y + d, 4) * 16 + zls * 4 + lax.rem(x + near, 4)
    row_b = lax.rem(y + near, 4) * 16 + (zls + 2) * 4 + lax.rem(x + d, 4)
    return jnp.where(ab == 0, row_a, row_b) * 3 + r


def kernel(
    tokens, gate_hbm, up_hbm, cot,
    hidden_out, token_out, GG, UG,
    S, tokb, TK, scr, X, Wt, gm, um, am_tx, am_rx, cotf,
    Pf, Ps, Pr, Qs, Qr, Ag, Ax, Asc, H, TS, TO, RT, scr2, R1s, R1r, R2f, R2s, R2r, acc, R3s, R3r, tscr,
    At,
    load_sem, tx, rx,
):
    zh, c, y, zl, x = position()
    sib = place(zh, 1 - c, y, zl, x)
    anti = place(1 - zh, c, y, zl, x)
    z = zh * 4 + zl

    def at_x(d):
        return place(zh, c, y, zl, lax.rem(x + d, 4))

    def at_y(d):
        return place(zh, c, lax.rem(y + d, 4), zl, x)

    def at_z(d):
        to = lax.rem(z + d, 8)
        return place(lax.div(to, 4), c, y, lax.rem(to, 4), x)

    xs_to, ys_to = [at_x(d) for d in (1, 2, 3)], [at_y(d) for d in (1, 2, 3)]
    zs_to = [at_z(d) for d in range(1, 8)]

    used = [0]
    copies = []

    def send(src, dst, to):
        i = used[0]
        used[0] += 1
        cp = pltpu.make_async_remote_copy(
            src_ref=src, dst_ref=dst, send_sem=tx.at[i], recv_sem=rx.at[i],
            device_id=to, device_id_type=MESH,
        )
        cp.start()
        copies.append(cp)
        return cp

    loads = []
    for i, (start, count) in enumerate(LOADS):
        rows = pl.ds(start, count)
        for k, (src, dst) in enumerate(((gate_hbm, gm), (up_hbm, um))):
            cp = pltpu.make_async_copy(src.at[rows], dst.at[rows], load_sem.at[i, k])
            cp.start()
            loads.append(cp)
    barrier = pltpu.get_barrier_semaphore()
    peers = [sib] + xs_to + ys_to + zs_to
    for p in peers:
        pl.semaphore_signal(barrier, inc=1, device_id=p, device_id_type=MESH)

    for j in range(64):
        tscr[pl.ds(j, 3, stride=64), :] = tokens[:, j * 128:(j + 1) * 128].astype(F32)
    for g in range(4):
        for r in range(3):
            tokb[g % 2, g // 2, r] = tscr[pl.ds(r * 64 + g * 16, 16), :].astype(BF16)

    tops = [jnp.zeros((16, DQ), BF16), jnp.zeros((16, DQ), BF16)]
    for i, (start, count) in enumerate(LOADS):
        for k, ref in enumerate((gm, um)):
            loads[2 * i + k].wait()

            def largest(b, top, ref=ref, start=start):
                rows = pl.ds(pl.multiple_of(start + b * 16, 16), 16)
                return jnp.maximum(top, jnp.abs(ref[rows, :]))

            tops[k] = lax.fori_loop(0, count // 16, largest, tops[k])
    for k in range(2):
        am_tx[0, pl.ds(8 * k, 8), :] = jnp.broadcast_to(
            jnp.max(tops[k].astype(F32), axis=(0, 1), keepdims=True), (8, 128)
        )

    pl.semaphore_wait(barrier, len(peers))

    t0 = send(tokb.at[1 - c], TK.at[:, c], sib)
    TK[:, c] = tokb[c]

    def share(stage, first, to):
        return [send(am_tx.at[stage], am_rx.at[first + i], p) for i, p in enumerate(to)]

    def merge(stage, first, cps):
        v = am_tx[stage]
        for i, cp in enumerate(cps):
            cp.wait_recv()
            v = jnp.maximum(v, am_rx[first + i])
        am_tx[stage + 1] = v

    m = share(0, 0, [sib])
    t0.wait_recv()
    near = S.at[lax.div(zl, 2), 0, lax.rem(zl, 2), zh]
    t1 = []
    for d, p in enumerate(zs_to):
        t1.append(send(TK.at[lax.div(lax.rem(z + d + 1, 8), 4)], near, p))
    near[...] = TK[zh]
    merge(0, 0, m)
    m = share(1, 1, xs_to)

    mine = absolute_row(lax.broadcasted_iota(jnp.int32, (192, 1), 0), y, x)
    col = lax.broadcasted_iota(jnp.int32, (192, 192), 1)
    pick = (col == mine).astype(F32).astype(BF16)
    cotf[...] = jnp.dot(pick, cot[...], preferred_element_type=F32)
    merge(1, 1, m)
    m = share(2, 4, ys_to)
    merge(2, 4, m)
    m = share(3, 7, zs_to)
    for cp in t1:
        cp.wait_recv()
    s2 = [[], []]
    for d in (1, 3, 2):
        s2[0].append(send(S.at[0, 0], S.at[0, d], at_x(4 - d)))
        s2[1].append(send(S.at[1, 0], S.at[1, d], at_y(4 - d)))
    merge(3, 7, m)

    g_amax = jnp.max(am_tx[4, 0:8, :], axis=(0, 1), keepdims=True)
    u_amax = jnp.max(am_tx[4, 8:16, :], axis=(0, 1), keepdims=True)
    g_factor, u_factor = QMAX / (g_amax + EPS), QMAX / (u_amax + EPS)
    g_scale, u_scale = (g_amax + EPS) / QMAX, (u_amax + EPS) / QMAX

    def quantized(ref, rows, factor):
        return jnp.floor(ref[rows, :].astype(F32) * factor + 0.5).astype(BF16)

    @pl.loop(0, FA // 16)
    def _(b):
        rows = pl.ds(pl.multiple_of(b * 16, 16), 16)
        Wt[rows, :] = quantized(gm, rows, g_factor)
        Wt[pl.ds(pl.multiple_of(FA + b * 16, 16), 16), :] = quantized(um, rows, u_factor)

    for t in range(0, FT, 16):
        Wt[2 * FA + t:2 * FA + t + 16, :] = quantized(gm, pl.ds(FA + t, 16), g_factor)
        Wt[2 * FA + FT + t:2 * FA + FT + t + 16, :] = quantized(um, pl.ds(FA + t, 16), u_factor)

    def far(ab):
        return at_y if ab == 0 else at_x

    for ab in range(2):
        for cp in s2[ab]:
            cp.wait_recv()
        scr[ab] = S[ab].reshape(1536, 128).astype(F32)
        for k in range(0, 12, 2):
            for fb in range(16):
                lo = scr[ab, pl.ds(SEAT[k] * 16 + fb, 8, stride=192), :]
                hi = scr[ab, pl.ds(SEAT[k + 1] * 16 + fb, 8, stride=192), :]
                at = ab * 96 + 8 * k
                X[0, at:at + 16, fb * 128:(fb + 1) * 128] = jnp.concatenate([lo, hi], axis=0).astype(BF16)

    big = {}

    def gather(q):
        big[q] = []
        for t, d in enumerate(FAR):
            for ab in range(2):
                own = pl.ds(ab * 96 + (q - 1) * 32, 32)
                there = pl.ds((ab * 3 + t) * 32, 32)
                big[q].append(send(X.at[0, own], X.at[q, there], far(ab)(4 - d)))

    p_copies, q_copies, sib_copies, anti_copies, fwd_copies = {}, {}, {}, {}, {}

    def forward(q):
        for n in range(0, FP, 256):
            width = min(256, FP - n)
            part = lax.dot_general(
                X[q], Wt[n:n + width, :], (((1,), (1,)), ((), ())), preferred_element_type=F32
            )
            for i in range(6):
                for k in range(4):
                    at = (i * 4 + k) * 8
                    Pf[q, k // 2, k % 2, i * 8:i * 8 + 8, n:n + width] = part[at:at + 8]
        Ps[q] = Pf[q, 1 - c].astype(BF16)
        p_copies[q] = send(Ps.at[q], Pr.at[q], sib)

    def cross(q):
        p_copies[q].wait_recv()
        Qs[q] = (Pf[q, c, 1 - zh] + Pr[q, 1 - zh].astype(F32)).astype(BF16)
        q_copies[q] = send(Qs.at[q], Qr.at[q], anti)

    def act(q):
        own = Pf[q, c, zh] + Pr[q, zh].astype(F32)
        q_copies[q].wait_recv()
        pre = own + Qr[q].astype(F32)
        gate = jnp.concatenate([pre[:, :FA], pre[:, 2 * FA:2 * FA + FT]], axis=1) * g_scale
        up = jnp.concatenate([pre[:, FA:2 * FA], pre[:, 2 * FA + FT:FP]], axis=1) * u_scale
        cotangent = cotf[q * 48:q * 48 + 48, :]
        sig = jax.nn.sigmoid(gate)
        silu = gate * sig
        H[q * 48:q * 48 + 48, :] = (silu * up).astype(BF16)
        ga = cotangent * up * sig * (1.0 + gate * (1.0 - sig))
        ua = cotangent * silu
        packed = jnp.concatenate([ga[:, :FA], ua[:, :FA], ga[:, FA:], ua[:, FA:]], axis=1)
        Ag[q, c, zh] = packed.astype(BF16)
        sib_copies[q] = send(Ag.at[q, c, zh], Ag.at[q, c, zh], sib)

    def cross_back(q):
        anti_copies[q] = send(Ag.at[q, c, zh], Ag.at[q, c, zh], anti)

    def pass_on(q):
        anti_copies[q].wait_recv()
        fwd_copies[q] = send(Ag.at[q, c, 1 - zh], Ag.at[q, c, 1 - zh], sib)

    lane = lax.broadcasted_iota(jnp.int32, (1, FP), 1)
    is_gate = (lane < FA) | ((lane >= 2 * FA) & (lane < 2 * FA + FT))
    scale_row = jnp.where(is_gate, g_scale, u_scale)
    rs = {}

    def backward(q):
        sib_copies[q].wait_recv()
        fwd_copies[q].wait_recv()
        parts = [Ag[q, k // 2, k % 2].astype(F32) for k in range(4)]
        rows = jnp.concatenate(
            [parts[k][i * 8:i * 8 + 8] for i in range(6) for k in range(4)], axis=0
        )
        Ax[q] = rows.astype(BF16)
        Asc[...] = (rows * scale_row).astype(BF16)
        for f in range(2):

            @pl.loop(0, 4)
            def _(j):
                cols = pl.ds(pl.multiple_of(j * 256, 256), 256)
                from_ = pl.ds(pl.multiple_of(f * 1024 + j * 256, 256), 256)
                part = jnp.dot(Asc[...], Wt[:, from_], preferred_element_type=F32)
                if q == 0:
                    TO[f, :, cols] = part
                else:
                    TS[q - 1, f, :, cols] = part.astype(BF16)

            if q == 3:
                scatter(q, f)
        if q in (1, 2):
            scatter(q, None)

    def scatter(q, f):
        fs = slice(None) if f is None else f
        rs[q, f] = []
        for t, d in enumerate(FAR):
            for ab in range(2):
                here = pl.ds((ab * 3 + t) * 32, 32)
                there = pl.ds((q - 1) * 32, 32)
                rs[q, f].append(
                    send(TS.at[q - 1, fs, here], RT.at[fs, ab, d - 1, there], far(ab)(d))
                )

    gather(1)
    forward(0)
    gather(2)
    cross(0)
    for cp in big[1]:
        cp.wait_recv()
    forward(1)
    gather(3)
    cross(1)
    act(0)
    cross_back(0)
    for cp in big[2]:
        cp.wait_recv()
    forward(2)
    cross(2)
    act(1)
    cross_back(1)
    for cp in big[3]:
        cp.wait_recv()
    forward(3)
    cross(3)
    pass_on(0)
    act(2)
    cross_back(2)
    backward(0)
    pass_on(1)
    backward(1)
    act(3)
    cross_back(3)
    pass_on(2)
    backward(2)
    pass_on(3)
    backward(3)

    def write_hidden():
        row = lax.broadcasted_iota(jnp.int32, (192, 192), 0)
        there = absolute_row(lax.broadcasted_iota(jnp.int32, (1, 192), 1), y, x)
        pick = (row == there).astype(F32).astype(BF16)
        hidden_out[...] = jnp.dot(pick, H[...], preferred_element_type=F32).astype(BF16)

    def transpose_acts():
        for i in range(6):
            At[:, i * 128:(i + 1) * 128] = Ax[...].reshape(768, FP)[i * 128:(i + 1) * 128, :].T

    def weight_grads(first, last):
        @pl.loop(first, last)
        def _(j):
            cols = pl.ds(pl.multiple_of(j * 256, 256), 256)
            part = jnp.dot(
                At[...], X[:, :, cols].reshape(768, 256), preferred_element_type=F32
            ).astype(BF16)
            GG[0:FA, cols] = part[0:FA]
            GG[FA:FW, cols] = part[2 * FA:2 * FA + FT]
            UG[0:FA, cols] = part[FA:2 * FA]
            UG[FA:FW, cols] = part[2 * FA + FT:FP]

    def near_scatter(r, arrived):
        for cp in arrived:
            cp.wait_recv()
        out = [[], []]
        there = slice(r * 32, r * 32 + 32)
        for ab in range(2):
            for f in range(2):
                for fb in range(8):
                    cols = slice(fb * 128, (fb + 1) * 128)
                    v = TO[f, ab * 96 + r * 32:ab * 96 + r * 32 + 32, cols]
                    for i in range(3):
                        v = v + RT[f, ab, i, there, cols].astype(F32)
                    for k in range(4):
                        seat = (k % 2) * 2 + k // 2
                        at = pl.ds(seat * 16 + f * 8 + fb, 8, stride=64)
                        scr2[r, ab, at, :] = v[8 * k:8 * k + 8]
            R1s[r, ab] = scr2[r, ab].astype(BF16).reshape(4, 128, 128)
            near_at = at_x if ab == 0 else at_y
            for d in FAR:
                out[ab].append(send(R1s.at[r, ab, d], R1r.at[r, ab, d - 1], near_at(d)))
        return out

    def column_scatter(r, r1):
        for ab in range(2):
            for cp in r1[ab]:
                cp.wait_recv()
            v = scr2[r, ab, 0:128, :]
            for i in range(3):
                v = v + R1r[r, ab, i].astype(F32)
            R2f[r, 2 * ab:2 * ab + 2] = v.reshape(2, 2, 32, 128)
            R2s[r, 2 * ab:2 * ab + 2] = v.astype(BF16).reshape(2, 2, 32, 128)
        out = []
        for d, p in enumerate(zs_to):
            to = lax.rem(z + d + 1, 8)
            out.append(send(R2s.at[r, lax.rem(to, 4), lax.div(to, 4)], R2r.at[r, d], p))
        return out

    def column_sum(r, r2):
        acc[r, zh] = R2f[r, zl, zh]
        acc[r, 1 - zh] = jnp.zeros((32, 128), F32)
        for d, cp in enumerate(r2):
            cp.wait_recv()
            half = lax.div(lax.rem(z + 7 - d, 8), 4)
            acc[r, half] = acc[r, half] + R2r[r, d].astype(F32)
        theirs = pl.ds(pl.multiple_of((1 - c) * 16, 16), 16)
        for h in range(2):
            R3s[r, h] = acc[r, h, theirs, :].astype(BF16)
            at = pl.ds(pl.multiple_of(r * 64 + (h * 2 + c) * 16, 16), 16)
            tscr[at, :] = acc[r, h, pl.ds(pl.multiple_of(c * 16, 16), 16), :]

    r1 = [near_scatter(0, rs[1, None]), near_scatter(1, rs[2, None])]
    transpose_acts()
    weight_grads(0, 2)
    r2 = [column_scatter(0, r1[0]), column_scatter(1, r1[1])]
    r1.append(near_scatter(2, rs[3, 0] + rs[3, 1]))
    weight_grads(2, 4)
    column_sum(0, r2[0])
    r2.append(column_scatter(2, r1[2]))
    column_sum(1, r2[1])
    weight_grads(4, 8)
    write_hidden()
    column_sum(2, r2[2])
    r3 = send(R3s, R3r, sib)
    r3.wait_recv()
    for r in range(3):
        for h in range(2):
            at = pl.ds(pl.multiple_of(r * 64 + (h * 2 + 1 - c) * 16, 16), 16)
            tscr[at, :] = R3r[r, h].astype(F32)
    for j in range(64):
        token_out[:, j * 128:(j + 1) * 128] = tscr[pl.ds(j, 3, stride=64), :].astype(BF16)

    for cp in copies:
        cp.wait_send()


def finish(*refs):
    n = len(refs) // 2
    sem = refs[-1]
    copies = [pltpu.make_async_copy(refs[i], refs[n + i], sem.at[i]) for i in range(n)]
    for cp in copies:
        cp.start()
    for cp in copies:
        cp.wait()


def on_device(tokens, gate_master, up_master, hidden_cotangent):
    vmem = pl.BlockSpec(memory_space=pltpu.VMEM)
    anywhere = pl.BlockSpec(memory_space=pl.ANY)
    V = pltpu.VMEM
    n_copies = 136
    shapes = ((192, FW), (3, 8192), (FW, DQ), (FW, DQ))
    results = pl.pallas_call(
        kernel,
        out_shape=tuple(V(shape, BF16) for shape in shapes),
        in_specs=[vmem, anywhere, anywhere, vmem],
        out_specs=(vmem,) * 4,
        scratch_shapes=[
            V((2, 4, 2, 2, 2, 3, 16, 128), BF16),
            V((2, 2, 3, 16, 128), BF16),
            V((2, 2, 3, 16, 128), BF16),
            V((2, 1536, 128), F32),
            V((4, 192, DQ), BF16),
            V((FP, DQ), BF16),
            V((FW, DQ), BF16),
            V((FW, DQ), BF16),
            V((5, 16, 128), F32),
            V((14, 16, 128), F32),
            V((192, FW), F32),
            V((4, 2, 2, 48, FP), F32),
            V((4, 2, 48, FP), BF16),
            V((4, 2, 48, FP), BF16),
            V((4, 48, FP), BF16),
            V((4, 48, FP), BF16),
            V((4, 2, 2, 48, FP), BF16),
            V((4, 192, FP), BF16),
            V((192, FP), BF16),
            V((192, FW), BF16),
            V((3, 2, 192, 1024), BF16),
            V((2, 192, 1024), F32),
            V((2, 2, 3, 96, 1024), BF16),
            V((3, 2, 512, 128), F32),
            V((3, 2, 4, 128, 128), BF16),
            V((3, 2, 3, 128, 128), BF16),
            V((3, 4, 2, 32, 128), F32),
            V((3, 4, 2, 32, 128), BF16),
            V((3, 7, 32, 128), BF16),
            V((3, 2, 32, 128), F32),
            V((3, 2, 16, 128), BF16),
            V((3, 2, 16, 128), BF16),
            V((192, 128), F32),
            V((FP, 768), BF16),
            pltpu.SemaphoreType.DMA((4, 2)),
            pltpu.SemaphoreType.DMA((n_copies,)),
            pltpu.SemaphoreType.DMA((n_copies,)),
        ],
        compiler_params=pltpu.CompilerParams(
            collective_id=0, has_side_effects=True, vmem_limit_bytes=36 * 2**20
        ),
        name="swiglu_step",
    )(
        tokens,
        pltpu.with_memory_space_constraint(gate_master.T, pltpu.HBM),
        pltpu.with_memory_space_constraint(up_master.T, pltpu.HBM),
        hidden_cotangent,
    )
    hidden, token_grad, gate_grad, up_grad = pl.pallas_call(
        finish,
        out_shape=tuple(jax.ShapeDtypeStruct(shape, BF16) for shape in shapes),
        in_specs=[vmem] * 4,
        out_specs=(anywhere,) * 4,
        scratch_shapes=[pltpu.SemaphoreType.DMA((4,))],
        compiler_params=pltpu.CompilerParams(vmem_limit_bytes=8 * 2**20),
        name="finish",
    )(*(pltpu.with_memory_space_constraint(r, pltpu.VMEM) for r in results))
    return hidden, token_grad, gate_grad.T, up_grad.T


def solution(mesh):
    placed = (
        P(("group", "fsdp"), None),
        P("group", "fsdp"),
        P("group", "fsdp"),
        P("group", "fsdp"),
    )
    return jax.shard_map(
        on_device,
        mesh=mesh,
        in_specs=placed,
        out_specs=(
            P("group", "fsdp"),
            P(("group", "fsdp"), None),
            P("group", "fsdp"),
            P("group", "fsdp"),
        ),
        check_vma=False,
    )
```

```python
import functools

import jax
import jax.numpy as jnp
from jax import lax
from jax.experimental import pallas as pl
from jax.experimental.pallas import tpu as pltpu
from jax.sharding import PartitionSpec as P

QMAX = 60.0
EPS = 1e-06
MESH = pl.DeviceIdType.MESH
F32 = jnp.float32
BF16 = jnp.bfloat16

DQ = 2048
FW = 416
FA = 384
FT = FW - FA
FP = 2 * FW
SEAT = tuple((k % 2) * 6 + (k // 2 % 2) * 3 + k // 4 for k in range(12))
LOADS = ((0, 112), (112, 112), (224, 96), (320, 96))
FAR = (1, 3, 2)


def position():
    g = lax.axis_index("group")
    f = lax.axis_index("fsdp")
    return lax.div(g, 2), lax.rem(g, 2), lax.div(f, 16), lax.rem(lax.div(f, 4), 4), lax.rem(f, 4)


def place(zh, c, y, zl, x):
    return {"group": zh * 2 + c, "fsdp": y * 16 + zl * 4 + x}


def absolute_row(n, y, x):
    chunk, i, u = lax.div(n, 48), lax.div(lax.rem(n, 48), 8), lax.rem(n, 8)
    ab, three = lax.div(i, 3), lax.rem(i, 3)
    near, zls = lax.div(u, 2), lax.rem(u, 2)
    d = jnp.where(chunk == 0, 0, jnp.where(three == 0, FAR[0], jnp.where(three == 1, FAR[1], FAR[2])))
    r = jnp.where(chunk == 0, three, chunk - 1)
    row_a = lax.rem(y + d, 4) * 16 + zls * 4 + lax.rem(x + near, 4)
    row_b = lax.rem(y + near, 4) * 16 + (zls + 2) * 4 + lax.rem(x + d, 4)
    return jnp.where(ab == 0, row_a, row_b) * 3 + r


def kernel(
    tokens_hbm, gate_hbm, up_hbm, cot_hbm,
    hidden_out, token_out, GG, UG,
    tokens, cot, S, tokb, TK, scr, X, Wt, gm, um, am_tx, am_rx, cotp, cotr, cotf,
    Pf, Ps, Pr, Q0s, Q0r, Qs, Qr, Ag, Ax, Asc, H, TS, TO, RT, scr2, R1s, R1r, R2f, R2s, R2r, acc, R3s, R3r, tscr,
    At,
    load_sem, in_sem, tx, rx,
):
    zh, c, y, zl, x = position()
    sib = place(zh, 1 - c, y, zl, x)
    anti = place(1 - zh, c, y, zl, x)
    z = zh * 4 + zl

    def at_x(d):
        return place(zh, c, y, zl, lax.rem(x + d, 4))

    def at_y(d):
        return place(zh, c, lax.rem(y + d, 4), zl, x)

    def at_z(d):
        to = lax.rem(z + d, 8)
        return place(lax.div(to, 4), c, y, lax.rem(to, 4), x)

    xs_to, ys_to = [at_x(d) for d in (1, 2, 3)], [at_y(d) for d in (1, 2, 3)]
    zs_to = [at_z(d) for d in range(1, 8)]

    used = [0]
    copies = []

    def send(src, dst, to):
        i = used[0]
        used[0] += 1
        cp = pltpu.make_async_remote_copy(
            src_ref=src, dst_ref=dst, send_sem=tx.at[i], recv_sem=rx.at[i],
            device_id=to, device_id_type=MESH,
        )
        cp.start()
        copies.append(cp)
        return cp

    small = []
    for i, (src, dst) in enumerate(((tokens_hbm, tokens), (cot_hbm, cot))):
        small.append(pltpu.make_async_copy(src, dst, in_sem.at[i]))
        small[i].start()
    loads = []
    for i, (start, count) in enumerate(LOADS):
        rows = pl.ds(start, count)
        for k, (src, dst) in enumerate(((gate_hbm, gm), (up_hbm, um))):
            cp = pltpu.make_async_copy(src.at[rows], dst.at[rows], load_sem.at[i, k])
            cp.start()
            loads.append(cp)
    barrier = pltpu.get_barrier_semaphore()
    peers = [sib] + xs_to + ys_to + zs_to
    for p in peers:
        pl.semaphore_signal(barrier, inc=1, device_id=p, device_id_type=MESH)

    small[0].wait()
    for j in range(64):
        tscr[pl.ds(j, 3, stride=64), :] = tokens[:, j * 128:(j + 1) * 128].astype(F32)
    for g in range(4):
        for r in range(3):
            tokb[g % 2, g // 2, r] = tscr[pl.ds(r * 64 + g * 16, 16), :].astype(BF16)

    tops = [jnp.zeros((16, DQ), BF16), jnp.zeros((16, DQ), BF16)]
    for i, (start, count) in enumerate(LOADS):
        for k, ref in enumerate((gm, um)):
            loads[2 * i + k].wait()

            def largest(b, top, ref=ref, start=start):
                rows = pl.ds(pl.multiple_of(start + b * 16, 16), 16)
                return jnp.maximum(top, jnp.abs(ref[rows, :]))

            tops[k] = lax.fori_loop(0, count // 16, largest, tops[k])
    for k in range(2):
        am_tx[0, pl.ds(8 * k, 8), :] = jnp.broadcast_to(
            jnp.max(tops[k].astype(F32), axis=(0, 1), keepdims=True), (8, 128)
        )

    pl.semaphore_wait(barrier, len(peers))

    t0 = send(tokb.at[1 - c], TK.at[:, c], sib)
    TK[:, c] = tokb[c]

    def share(stage, first, to):
        return [send(am_tx.at[stage], am_rx.at[first + i], p) for i, p in enumerate(to)]

    def merge(stage, first, cps):
        v = am_tx[stage]
        for i, cp in enumerate(cps):
            cp.wait_recv()
            v = jnp.maximum(v, am_rx[first + i])
        am_tx[stage + 1] = v

    m = share(0, 0, [sib])
    t0.wait_recv()
    near = S.at[lax.div(zl, 2), 0, lax.rem(zl, 2), zh]
    t1 = []
    for d, p in enumerate(zs_to):
        t1.append(send(TK.at[lax.div(lax.rem(z + d + 1, 8), 4)], near, p))
    near[...] = TK[zh]
    merge(0, 0, m)
    m = share(1, 1, xs_to)

    small[1].wait()
    mine = absolute_row(lax.broadcasted_iota(jnp.int32, (192, 1), 0), y, x)
    col = lax.broadcasted_iota(jnp.int32, (192, 192), 1)
    pick = (col == mine).astype(F32).astype(BF16)
    cperm = jnp.dot(pick, cot[...], preferred_element_type=F32)
    cotf[zh] = cperm
    cotp[...] = cperm.astype(BF16)
    merge(1, 1, m)
    m = share(2, 4, ys_to)
    merge(2, 4, m)
    m = share(3, 7, zs_to)
    for cp in t1:
        cp.wait_recv()
    s2 = [[], []]
    for d in (1, 3, 2):
        s2[0].append(send(S.at[0, 0], S.at[0, d], at_x(4 - d)))
        s2[1].append(send(S.at[1, 0], S.at[1, d], at_y(4 - d)))
    merge(3, 7, m)
    remote = pl.ds(48, 144)
    cot_copy = send(cotp.at[remote], cotr.at[remote], anti)

    g_amax = jnp.max(am_tx[4, 0:8, :], axis=(0, 1), keepdims=True)
    u_amax = jnp.max(am_tx[4, 8:16, :], axis=(0, 1), keepdims=True)
    g_factor, u_factor = QMAX / (g_amax + EPS), QMAX / (u_amax + EPS)
    g_scale, u_scale = (g_amax + EPS) / QMAX, (u_amax + EPS) / QMAX

    def quantized(ref, rows, factor):
        return jnp.floor(ref[rows, :].astype(F32) * factor + 0.5).astype(BF16)

    @pl.loop(0, FA // 16)
    def _(b):
        rows = pl.ds(pl.multiple_of(b * 16, 16), 16)
        Wt[rows, :] = quantized(gm, rows, g_factor)
        Wt[pl.ds(pl.multiple_of(FA + b * 16, 16), 16), :] = quantized(um, rows, u_factor)

    for t in range(0, FT, 16):
        Wt[2 * FA + t:2 * FA + t + 16, :] = quantized(gm, pl.ds(FA + t, 16), g_factor)
        Wt[2 * FA + FT + t:2 * FA + FT + t + 16, :] = quantized(um, pl.ds(FA + t, 16), u_factor)

    def far(ab):
        return at_y if ab == 0 else at_x

    for ab in range(2):
        for cp in s2[ab]:
            cp.wait_recv()
        scr[ab] = S[ab].reshape(1536, 128).astype(F32)
        for k in range(0, 12, 2):
            for fb in range(16):
                lo = scr[ab, pl.ds(SEAT[k] * 16 + fb, 8, stride=192), :]
                hi = scr[ab, pl.ds(SEAT[k + 1] * 16 + fb, 8, stride=192), :]
                at = ab * 96 + 8 * k
                X[0, at:at + 16, fb * 128:(fb + 1) * 128] = jnp.concatenate([lo, hi], axis=0).astype(BF16)

    big = {}

    def gather(q):
        big[q] = []
        for t, d in enumerate(FAR):
            for ab in range(2):
                own = pl.ds(ab * 96 + (q - 1) * 32, 32)
                there = pl.ds((ab * 3 + t) * 32, 32)
                big[q].append(send(X.at[0, own], X.at[q, there], far(ab)(4 - d)))

    p_copies, q_copies, sib_copies, anti_copies, fwd_copies = {}, {}, {}, {}, {}

    def forward(q):
        for n in range(0, FP, 256):
            width = min(256, FP - n)
            part = lax.dot_general(
                X[q], Wt[n:n + width, :], (((1,), (1,)), ((), ())), preferred_element_type=F32
            )
            for i in range(6):
                for k in range(4):
                    at = (i * 4 + k) * 8
                    Pf[q, k // 2, k % 2, i * 8:i * 8 + 8, n:n + width] = part[at:at + 8]
        Ps[q] = Pf[q, 1 - c].astype(BF16)
        p_copies[q] = send(Ps.at[q], Pr.at[q], sib)

    def cross(q):
        p_copies[q].wait_recv()
        if q == 0:
            Q0s[...] = (Pf[q, c, 1 - zh] + Pr[q, 1 - zh].astype(F32)).astype(BF16)
            q_copies[q] = send(Q0s, Q0r, anti)
        else:
            tails = []
            for h in range(2):
                v = Pf[q, c, h] + Pr[q, h].astype(F32)
                for j in range(6):
                    Qs[q - 1, h * 6 + j] = v[:, j * 128:(j + 1) * 128].astype(BF16)
                tails.append(v[:, 2 * FA:])
            Qs[q - 1, 12] = jnp.concatenate(tails, axis=1).astype(BF16)
            q_copies[q] = send(Qs.at[q - 1], Qr.at[q - 1], anti)

    def act_rows(q, h):
        pre = Pf[q, c, h] + Pr[q, h].astype(F32)
        if q == 0:
            pre = pre + Q0r[...].astype(F32)
        else:
            tail = Qr[q - 1, 12].astype(F32)[:, h * 2 * FT:(h + 1) * 2 * FT]
            tiles = [Qr[q - 1, h * 6 + j].astype(F32) for j in range(6)]
            pre = pre + jnp.concatenate(tiles + [tail], axis=1)
        gate = jnp.concatenate([pre[:, :FA], pre[:, 2 * FA:2 * FA + FT]], axis=1) * g_scale
        up = jnp.concatenate([pre[:, FA:2 * FA], pre[:, 2 * FA + FT:FP]], axis=1) * u_scale
        cotangent = cotf[h, q * 48:q * 48 + 48, :]
        sig = jax.nn.sigmoid(gate)
        silu = gate * sig
        H[h, q * 48:q * 48 + 48, :] = (silu * up).astype(BF16)
        ga = cotangent * up * sig * (1.0 + gate * (1.0 - sig))
        ua = cotangent * silu
        packed = jnp.concatenate([ga[:, :FA], ua[:, :FA], ga[:, FA:], ua[:, FA:]], axis=1)
        Ag[q, c, h] = packed.astype(BF16)

    def act(q):
        q_copies[q].wait_recv()
        if q == 0:
            act_rows(q, zh)
            sib_copies[q] = send(Ag.at[q, c, zh], Ag.at[q, c, zh], sib)
        else:
            for h in range(2):
                act_rows(q, h)
            sib_copies[q] = send(Ag.at[q, c], Ag.at[q, c], sib)

    def cross_back(q):
        anti_copies[q] = send(Ag.at[q, c, zh], Ag.at[q, c, zh], anti)

    def pass_on(q):
        anti_copies[q].wait_recv()
        fwd_copies[q] = send(Ag.at[q, c, 1 - zh], Ag.at[q, c, 1 - zh], sib)

    lane = lax.broadcasted_iota(jnp.int32, (1, FP), 1)
    is_gate = (lane < FA) | ((lane >= 2 * FA) & (lane < 2 * FA + FT))
    scale_row = jnp.where(is_gate, g_scale, u_scale)
    rs = {}

    def backward(q):
        sib_copies[q].wait_recv()
        if q == 0:
            fwd_copies[q].wait_recv()
        parts = [Ag[q, k // 2, k % 2].astype(F32) for k in range(4)]
        rows = jnp.concatenate(
            [parts[k][i * 8:i * 8 + 8] for i in range(6) for k in range(4)], axis=0
        )
        Ax[q] = rows.astype(BF16)
        Asc[...] = (rows * scale_row).astype(BF16)
        for f in range(2):

            @pl.loop(0, 4)
            def _(j):
                cols = pl.ds(pl.multiple_of(j * 256, 256), 256)
                from_ = pl.ds(pl.multiple_of(f * 1024 + j * 256, 256), 256)
                part = jnp.dot(Asc[...], Wt[:, from_], preferred_element_type=F32)
                if q == 0:
                    TO[f, :, cols] = part
                else:
                    TS[q - 1, f, :, cols] = part.astype(BF16)

            if q == 3:
                scatter(q, f)
        if q in (1, 2):
            scatter(q, None)

    def scatter(q, f):
        fs = slice(None) if f is None else f
        rs[q, f] = []
        for t, d in enumerate(FAR):
            for ab in range(2):
                here = pl.ds((ab * 3 + t) * 32, 32)
                there = pl.ds((q - 1) * 32, 32)
                rs[q, f].append(
                    send(TS.at[q - 1, fs, here], RT.at[fs, ab, d - 1, there], far(ab)(d))
                )

    def transpose_acts(blocks):
        for i in blocks:
            At[:, i * 128:(i + 1) * 128] = Ax[...].reshape(768, FP)[i * 128:(i + 1) * 128, :].T

    gather(1)
    forward(0)
    gather(2)
    cross(0)
    for cp in big[1]:
        cp.wait_recv()
    forward(1)
    gather(3)
    cross(1)
    act(0)
    for cp in big[2]:
        cp.wait_recv()
    forward(2)
    cross(2)
    cot_copy.wait_recv()
    cotf[1 - zh, remote, :] = cotr[remote, :].astype(F32)
    act(1)
    for cp in big[3]:
        cp.wait_recv()
    forward(3)
    cross(3)
    cross_back(0)
    backward(1)
    act(2)
    backward(2)
    transpose_acts((2, 3))
    act(3)
    backward(3)
    pass_on(0)
    backward(0)

    def write_hidden():
        row = lax.broadcasted_iota(jnp.int32, (192, 192), 0)
        there = absolute_row(lax.broadcasted_iota(jnp.int32, (1, 192), 1), y, x)
        pick = (row == there).astype(F32).astype(BF16)
        hidden_out[...] = jnp.dot(pick, H[zh], preferred_element_type=F32).astype(BF16)

    def weight_grads(first, last):
        @pl.loop(first, last)
        def _(j):
            cols = pl.ds(pl.multiple_of(j * 256, 256), 256)
            part = jnp.dot(
                At[...], X[:, :, cols].reshape(768, 256), preferred_element_type=F32
            ).astype(BF16)
            GG[0:FA, cols] = part[0:FA]
            GG[FA:FW, cols] = part[2 * FA:2 * FA + FT]
            UG[0:FA, cols] = part[FA:2 * FA]
            UG[FA:FW, cols] = part[2 * FA + FT:FP]

    def near_scatter(r, arrived):
        for cp in arrived:
            cp.wait_recv()
        out = [[], []]
        there = slice(r * 32, r * 32 + 32)
        for ab in range(2):
            for f in range(2):
                for fb in range(8):
                    cols = slice(fb * 128, (fb + 1) * 128)
                    v = TO[f, ab * 96 + r * 32:ab * 96 + r * 32 + 32, cols]
                    for i in range(3):
                        v = v + RT[f, ab, i, there, cols].astype(F32)
                    for k in range(4):
                        seat = (k % 2) * 2 + k // 2
                        at = pl.ds(seat * 16 + f * 8 + fb, 8, stride=64)
                        scr2[r, ab, at, :] = v[8 * k:8 * k + 8]
            R1s[r, ab] = scr2[r, ab].astype(BF16).reshape(4, 128, 128)
            near_at = at_x if ab == 0 else at_y
            for d in FAR:
                out[ab].append(send(R1s.at[r, ab, d], R1r.at[r, ab, d - 1], near_at(d)))
        return out

    def column_scatter(r, r1):
        for ab in range(2):
            for cp in r1[ab]:
                cp.wait_recv()
            v = scr2[r, ab, 0:128, :]
            for i in range(3):
                v = v + R1r[r, ab, i].astype(F32)
            R2f[r, 2 * ab:2 * ab + 2] = v.reshape(2, 2, 32, 128)
            R2s[r, 2 * ab:2 * ab + 2] = v.astype(BF16).reshape(2, 2, 32, 128)
        out = []
        for d, p in enumerate(zs_to):
            to = lax.rem(z + d + 1, 8)
            out.append(send(R2s.at[r, lax.rem(to, 4), lax.div(to, 4)], R2r.at[r, d], p))
        return out

    def column_sum(r, r2):
        acc[r, zh] = R2f[r, zl, zh]
        acc[r, 1 - zh] = jnp.zeros((32, 128), F32)
        for d, cp in enumerate(r2):
            cp.wait_recv()
            half = lax.div(lax.rem(z + 7 - d, 8), 4)
            acc[r, half] = acc[r, half] + R2r[r, d].astype(F32)
        theirs = pl.ds(pl.multiple_of((1 - c) * 16, 16), 16)
        for h in range(2):
            R3s[r, h] = acc[r, h, theirs, :].astype(BF16)
            at = pl.ds(pl.multiple_of(r * 64 + (h * 2 + c) * 16, 16), 16)
            tscr[at, :] = acc[r, h, pl.ds(pl.multiple_of(c * 16, 16), 16), :]

    r1 = [near_scatter(0, rs[1, None]), near_scatter(1, rs[2, None])]
    transpose_acts((0, 1, 4, 5))
    weight_grads(0, 3)
    r2 = [column_scatter(0, r1[0])]
    r1.append(near_scatter(2, rs[3, 0] + rs[3, 1]))
    r2.append(column_scatter(1, r1[1]))
    weight_grads(3, 6)
    r2.append(column_scatter(2, r1[2]))
    column_sum(0, r2[0])
    weight_grads(6, 8)
    write_hidden()
    column_sum(1, r2[1])
    column_sum(2, r2[2])
    r3 = send(R3s, R3r, sib)
    r3.wait_recv()
    for r in range(3):
        for h in range(2):
            at = pl.ds(pl.multiple_of(r * 64 + (h * 2 + 1 - c) * 16, 16), 16)
            tscr[at, :] = R3r[r, h].astype(F32)
    for j in range(64):
        token_out[:, j * 128:(j + 1) * 128] = tscr[pl.ds(j, 3, stride=64), :].astype(BF16)

    for cp in copies:
        cp.wait_send()


def finish(*refs):
    n = len(refs) // 2
    sem = refs[-1]
    copies = [pltpu.make_async_copy(refs[i], refs[n + i], sem.at[i]) for i in range(n)]
    for cp in copies:
        cp.start()
    for cp in copies:
        cp.wait()


def on_device(tokens, gate_master, up_master, hidden_cotangent):
    vmem = pl.BlockSpec(memory_space=pltpu.VMEM)
    anywhere = pl.BlockSpec(memory_space=pl.ANY)
    V = pltpu.VMEM
    n_copies = 136
    shapes = ((192, FW), (3, 8192), (FW, DQ), (FW, DQ))
    results = pl.pallas_call(
        kernel,
        out_shape=tuple(V(shape, BF16) for shape in shapes),
        in_specs=[anywhere] * 4,
        out_specs=(vmem,) * 4,
        scratch_shapes=[
            V((3, 8192), BF16),
            V((192, FW), BF16),
            V((2, 4, 2, 2, 2, 3, 16, 128), BF16),
            V((2, 2, 3, 16, 128), BF16),
            V((2, 2, 3, 16, 128), BF16),
            V((2, 1536, 128), F32),
            V((4, 192, DQ), BF16),
            V((FP, DQ), BF16),
            V((FW, DQ), BF16),
            V((FW, DQ), BF16),
            V((5, 16, 128), F32),
            V((14, 16, 128), F32),
            V((192, FW), BF16),
            V((192, FW), BF16),
            V((2, 192, FW), F32),
            V((4, 2, 2, 48, FP), F32),
            V((4, 2, 48, FP), BF16),
            V((4, 2, 48, FP), BF16),
            V((48, FP), BF16),
            V((48, FP), BF16),
            V((3, 13, 48, 128), BF16),
            V((3, 13, 48, 128), BF16),
            V((4, 2, 2, 48, FP), BF16),
            V((4, 192, FP), BF16),
            V((192, FP), BF16),
            V((2, 192, FW), BF16),
            V((3, 2, 192, 1024), BF16),
            V((2, 192, 1024), F32),
            V((2, 2, 3, 96, 1024), BF16),
            V((3, 2, 512, 128), F32),
            V((3, 2, 4, 128, 128), BF16),
            V((3, 2, 3, 128, 128), BF16),
            V((3, 4, 2, 32, 128), F32),
            V((3, 4, 2, 32, 128), BF16),
            V((3, 7, 32, 128), BF16),
            V((3, 2, 32, 128), F32),
            V((3, 2, 16, 128), BF16),
            V((3, 2, 16, 128), BF16),
            V((192, 128), F32),
            V((FP, 768), BF16),
            pltpu.SemaphoreType.DMA((4, 2)),
            pltpu.SemaphoreType.DMA((2,)),
            pltpu.SemaphoreType.DMA((n_copies,)),
            pltpu.SemaphoreType.DMA((n_copies,)),
        ],
        compiler_params=pltpu.CompilerParams(
            collective_id=0, has_side_effects=True, vmem_limit_bytes=36 * 2**20
        ),
        name="swiglu_step",
    )(
        *(
            pltpu.with_memory_space_constraint(a, pltpu.HBM)
            for a in (tokens, gate_master.T, up_master.T, hidden_cotangent)
        )
    )
    hidden, token_grad, gate_grad, up_grad = pl.pallas_call(
        finish,
        out_shape=tuple(jax.ShapeDtypeStruct(shape, BF16) for shape in shapes),
        in_specs=[vmem] * 4,
        out_specs=(anywhere,) * 4,
        scratch_shapes=[pltpu.SemaphoreType.DMA((4,))],
        compiler_params=pltpu.CompilerParams(vmem_limit_bytes=8 * 2**20),
        name="finish",
    )(*(pltpu.with_memory_space_constraint(r, pltpu.VMEM) for r in results))
    return hidden, token_grad, gate_grad.T, up_grad.T


def solution(mesh):
    placed = (
        P(("group", "fsdp"), None),
        P("group", "fsdp"),
        P("group", "fsdp"),
        P("group", "fsdp"),
    )
    return jax.shard_map(
        on_device,
        mesh=mesh,
        in_specs=placed,
        out_specs=(
            P("group", "fsdp"),
            P(("group", "fsdp"), None),
            P("group", "fsdp"),
            P("group", "fsdp"),
        ),
        check_vma=False,
    )
```

```python
import functools

import jax
import jax.numpy as jnp
from jax import lax
from jax.experimental import pallas as pl
from jax.experimental.pallas import tpu as pltpu
from jax.sharding import PartitionSpec as P

QMAX = 60.0
EPS = 1e-06
MESH = pl.DeviceIdType.MESH
F32 = jnp.float32
BF16 = jnp.bfloat16

DQ = 2048
FW = 416
FA = 384
FT = FW - FA
FP = 2 * FW
SEAT = tuple((k % 2) * 6 + (k // 2 % 2) * 3 + k // 4 for k in range(12))
LOADS = ((0, 112), (112, 112), (224, 96), (320, 96))
FAR = (1, 3, 2)


def position():
    g = lax.axis_index("group")
    f = lax.axis_index("fsdp")
    return lax.div(g, 2), lax.rem(g, 2), lax.div(f, 16), lax.rem(lax.div(f, 4), 4), lax.rem(f, 4)


def place(zh, c, y, zl, x):
    return {"group": zh * 2 + c, "fsdp": y * 16 + zl * 4 + x}


def absolute_row(n, y, x):
    chunk, i, u = lax.div(n, 48), lax.div(lax.rem(n, 48), 8), lax.rem(n, 8)
    own = chunk == 0
    ab = jnp.where(own, lax.div(i, 3), lax.rem(i, 2))
    three = jnp.where(own, lax.rem(i, 3), lax.div(i, 2))
    near, zls = lax.div(u, 2), lax.rem(u, 2)
    d = jnp.where(own, 0, jnp.where(three == 0, FAR[0], jnp.where(three == 1, FAR[1], FAR[2])))
    r = jnp.where(own, three, chunk - 1)
    row_a = lax.rem(y + d, 4) * 16 + zls * 4 + lax.rem(x + near, 4)
    row_b = lax.rem(y + near, 4) * 16 + (zls + 2) * 4 + lax.rem(x + d, 4)
    return jnp.where(ab == 0, row_a, row_b) * 3 + r


def kernel(
    tokens_hbm, gate_hbm, up_hbm, cot_hbm,
    hidden_out, token_out, GG, UG,
    tokens, cot, S, tokb, TK, scr, X, Wt, gm, um, am_tx, am_rx, cotp, cotr, cotf,
    Pf, Ps, Pr, Q0s, Q0r, Qs, Qr, Ag, Ax, Asc, H, TS, TO, RT, scr2, R1s, R1r, R2f, R2s, R2r, acc, R3s, R3r, tscr,
    At,
    load_sem, in_sem, tx, rx,
):
    zh, c, y, zl, x = position()
    sib = place(zh, 1 - c, y, zl, x)
    anti = place(1 - zh, c, y, zl, x)
    z = zh * 4 + zl

    def at_x(d):
        return place(zh, c, y, zl, lax.rem(x + d, 4))

    def at_y(d):
        return place(zh, c, lax.rem(y + d, 4), zl, x)

    def at_z(d):
        to = lax.rem(z + d, 8)
        return place(lax.div(to, 4), c, y, lax.rem(to, 4), x)

    xs_to, ys_to = [at_x(d) for d in (1, 2, 3)], [at_y(d) for d in (1, 2, 3)]
    zs_to = [at_z(d) for d in range(1, 8)]

    used = [0]
    copies = []

    def send(src, dst, to):
        i = used[0]
        used[0] += 1
        cp = pltpu.make_async_remote_copy(
            src_ref=src, dst_ref=dst, send_sem=tx.at[i], recv_sem=rx.at[i],
            device_id=to, device_id_type=MESH,
        )
        cp.start()
        copies.append(cp)
        return cp

    small = []
    for i, (src, dst) in enumerate(((tokens_hbm, tokens), (cot_hbm, cot))):
        small.append(pltpu.make_async_copy(src, dst, in_sem.at[i]))
        small[i].start()
    loads = []
    for i, (start, count) in enumerate(LOADS):
        rows = pl.ds(start, count)
        for k, (src, dst) in enumerate(((gate_hbm, gm), (up_hbm, um))):
            cp = pltpu.make_async_copy(src.at[rows], dst.at[rows], load_sem.at[i, k])
            cp.start()
            loads.append(cp)
    barrier = pltpu.get_barrier_semaphore()
    peers = [sib] + xs_to + ys_to + zs_to
    for p in peers:
        pl.semaphore_signal(barrier, inc=1, device_id=p, device_id_type=MESH)

    small[0].wait()
    for j in range(64):
        tscr[pl.ds(j, 3, stride=64), :] = tokens[:, j * 128:(j + 1) * 128].astype(F32)
    for g in range(4):
        for r in range(3):
            tokb[g % 2, g // 2, r] = tscr[pl.ds(r * 64 + g * 16, 16), :].astype(BF16)

    tops = [jnp.zeros((16, DQ), BF16), jnp.zeros((16, DQ), BF16)]
    for i, (start, count) in enumerate(LOADS):
        for k, ref in enumerate((gm, um)):
            loads[2 * i + k].wait()

            def largest(b, top, ref=ref, start=start):
                rows = pl.ds(pl.multiple_of(start + b * 16, 16), 16)
                return jnp.maximum(top, jnp.abs(ref[rows, :]))

            tops[k] = lax.fori_loop(0, count // 16, largest, tops[k])
    for k in range(2):
        am_tx[0, pl.ds(8 * k, 8), :] = jnp.broadcast_to(
            jnp.max(tops[k].astype(F32), axis=(0, 1), keepdims=True), (8, 128)
        )

    pl.semaphore_wait(barrier, len(peers))

    t0 = send(tokb.at[1 - c], TK.at[:, c], sib)
    TK[:, c] = tokb[c]

    def share(stage, first, to):
        return [send(am_tx.at[stage], am_rx.at[first + i], p) for i, p in enumerate(to)]

    def merge(stage, first, cps):
        v = am_tx[stage]
        for i, cp in enumerate(cps):
            cp.wait_recv()
            v = jnp.maximum(v, am_rx[first + i])
        am_tx[stage + 1] = v

    m = share(0, 0, [sib])
    t0.wait_recv()
    near = S.at[lax.div(zl, 2), 0, lax.rem(zl, 2), zh]
    t1 = []
    for d, p in enumerate(zs_to):
        t1.append(send(TK.at[lax.div(lax.rem(z + d + 1, 8), 4)], near, p))
    near[...] = TK[zh]
    merge(0, 0, m)
    m = share(1, 1, xs_to)

    small[1].wait()
    mine = absolute_row(lax.broadcasted_iota(jnp.int32, (192, 1), 0), y, x)
    col = lax.broadcasted_iota(jnp.int32, (192, 192), 1)
    pick = (col == mine).astype(F32).astype(BF16)
    cperm = jnp.dot(pick, cot[...], preferred_element_type=F32)
    cotf[zh] = cperm
    cotp[...] = cperm.astype(BF16)
    merge(1, 1, m)
    m = share(2, 4, ys_to)
    merge(2, 4, m)
    m = share(3, 7, zs_to)
    for cp in t1:
        cp.wait_recv()
    s2 = [[], []]
    for d in (1, 3, 2):
        s2[0].append(send(S.at[0, 0], S.at[0, d], at_x(4 - d)))
        s2[1].append(send(S.at[1, 0], S.at[1, d], at_y(4 - d)))
    merge(3, 7, m)
    remote = pl.ds(48, 144)
    cot_copy = send(cotp.at[remote], cotr.at[remote], anti)

    g_amax = jnp.max(am_tx[4, 0:8, :], axis=(0, 1), keepdims=True)
    u_amax = jnp.max(am_tx[4, 8:16, :], axis=(0, 1), keepdims=True)
    g_factor, u_factor = QMAX / (g_amax + EPS), QMAX / (u_amax + EPS)
    g_scale, u_scale = (g_amax + EPS) / QMAX, (u_amax + EPS) / QMAX

    def quantized(ref, rows, factor):
        return jnp.floor(ref[rows, :].astype(F32) * factor + 0.5).astype(BF16)

    @pl.loop(0, FA // 16)
    def _(b):
        rows = pl.ds(pl.multiple_of(b * 16, 16), 16)
        Wt[rows, :] = quantized(gm, rows, g_factor)
        Wt[pl.ds(pl.multiple_of(FA + b * 16, 16), 16), :] = quantized(um, rows, u_factor)

    for t in range(0, FT, 16):
        Wt[2 * FA + t:2 * FA + t + 16, :] = quantized(gm, pl.ds(FA + t, 16), g_factor)
        Wt[2 * FA + FT + t:2 * FA + FT + t + 16, :] = quantized(um, pl.ds(FA + t, 16), u_factor)

    def far(ab):
        return at_y if ab == 0 else at_x

    for ab in range(2):
        for cp in s2[ab]:
            cp.wait_recv()
        scr[ab] = S[ab].reshape(1536, 128).astype(F32)
        for k in range(0, 12, 2):
            for fb in range(16):
                lo = scr[ab, pl.ds(SEAT[k] * 16 + fb, 8, stride=192), :]
                hi = scr[ab, pl.ds(SEAT[k + 1] * 16 + fb, 8, stride=192), :]
                at = ab * 96 + 8 * k
                X[0, at:at + 16, fb * 128:(fb + 1) * 128] = jnp.concatenate([lo, hi], axis=0).astype(BF16)

    big = {}

    def gather(q):
        big[q] = []
        for t, d in enumerate(FAR):
            for ab in range(2):
                own = pl.ds(ab * 96 + (q - 1) * 32, 32)
                there = pl.ds((t * 2 + ab) * 32, 32)
                big[q].append(send(X.at[0, own], X.at[q, there], far(ab)(4 - d)))

    p_copies, q_copies, sib_copies, anti_copies, fwd_copies = {}, {}, {}, {}, {}

    def forward(q, first=0, last=6):
        if q > 0:
            for cp in big[q][first:last]:
                cp.wait_recv()
        for n in range(0, FP, 256):
            width = min(256, FP - n)
            part = lax.dot_general(
                X[q, first * 32:last * 32, :], Wt[n:n + width, :],
                (((1,), (1,)), ((), ())), preferred_element_type=F32,
            )
            for i in range(first, last):
                for k in range(4):
                    at = ((i - first) * 4 + k) * 8
                    Pf[q, k // 2, k % 2, i * 8:i * 8 + 8, n:n + width] = part[at:at + 8]
        rows = pl.ds(first * 8, (last - first) * 8)
        Ps[q, :, rows, :] = Pf[q, 1 - c, :, rows, :].astype(BF16)
        p_copies[q, first] = send(Ps.at[q, :, rows], Pr.at[q, :, rows], sib)

    def cross(q, first=0, last=6):
        p_copies[q, first].wait_recv()
        rows = pl.ds(first * 8, (last - first) * 8)
        if q == 0:
            Q0s[...] = (Pf[q, c, 1 - zh] + Pr[q, 1 - zh].astype(F32)).astype(BF16)
            q_copies[q, first] = send(Q0s, Q0r, anti)
        else:
            tails = []
            for h in range(2):
                v = Pf[q, c, h, rows, :] + Pr[q, h, rows, :].astype(F32)
                for j in range(6):
                    Qs[q - 1, h * 6 + j, rows, :] = v[:, j * 128:(j + 1) * 128].astype(BF16)
                tails.append(v[:, 2 * FA:])
            Qs[q - 1, 12, rows, :] = jnp.concatenate(tails, axis=1).astype(BF16)
            q_copies[q, first] = send(Qs.at[q - 1, :, rows], Qr.at[q - 1, :, rows], anti)

    def act_rows(q, h, first, last):
        rows = pl.ds(first * 8, (last - first) * 8)
        pre = Pf[q, c, h, rows, :] + Pr[q, h, rows, :].astype(F32)
        if q == 0:
            pre = pre + Q0r[...].astype(F32)
        else:
            tail = Qr[q - 1, 12, rows, :].astype(F32)[:, h * 2 * FT:(h + 1) * 2 * FT]
            tiles = [Qr[q - 1, h * 6 + j, rows, :].astype(F32) for j in range(6)]
            pre = pre + jnp.concatenate(tiles + [tail], axis=1)
        gate = jnp.concatenate([pre[:, :FA], pre[:, 2 * FA:2 * FA + FT]], axis=1) * g_scale
        up = jnp.concatenate([pre[:, FA:2 * FA], pre[:, 2 * FA + FT:FP]], axis=1) * u_scale
        mine = pl.ds(q * 48 + first * 8, (last - first) * 8)
        cotangent = cotf[h, mine, :]
        sig = jax.nn.sigmoid(gate)
        silu = gate * sig
        H[h, mine, :] = (silu * up).astype(BF16)
        ga = cotangent * up * sig * (1.0 + gate * (1.0 - sig))
        ua = cotangent * silu
        packed = jnp.concatenate([ga[:, :FA], ua[:, :FA], ga[:, FA:], ua[:, FA:]], axis=1)
        Ag[q, c, h, rows, :] = packed.astype(BF16)

    def act(q, first=0, last=6):
        q_copies[q, first].wait_recv()
        if q == 0:
            act_rows(q, zh, first, last)
            mine = Ag.at[q, c, zh]
        else:
            for h in range(2):
                act_rows(q, h, first, last)
            mine = Ag.at[q, c, :, pl.ds(first * 8, (last - first) * 8)]
        sib_copies[q, first] = send(mine, mine, sib)

    def cross_back(q):
        anti_copies[q] = send(Ag.at[q, c, zh], Ag.at[q, c, zh], anti)

    def pass_on(q):
        anti_copies[q].wait_recv()
        fwd_copies[q] = send(Ag.at[q, c, 1 - zh], Ag.at[q, c, 1 - zh], sib)

    lane = lax.broadcasted_iota(jnp.int32, (1, FP), 1)
    is_gate = (lane < FA) | ((lane >= 2 * FA) & (lane < 2 * FA + FT))
    scale_row = jnp.where(is_gate, g_scale, u_scale)
    rs = {1: [], 2: [], 3: []}

    def backward(q, first=0, last=6):
        for f in range(first, last):
            if (q, f) in sib_copies:
                sib_copies[q, f].wait_recv()
        if q == 0:
            fwd_copies[q].wait_recv()
        mine = pl.ds(first * 8, (last - first) * 8)
        parts = [Ag[q, k // 2, k % 2, mine, :].astype(F32) for k in range(4)]
        rows = jnp.concatenate(
            [parts[k][i * 8:i * 8 + 8] for i in range(last - first) for k in range(4)], axis=0
        )
        here = pl.ds(first * 32, (last - first) * 32)
        Ax[q, here, :] = rows.astype(BF16)
        Asc[here, :] = (rows * scale_row).astype(BF16)
        for f in range(2):

            @pl.loop(0, 4)
            def _(j):
                cols = pl.ds(pl.multiple_of(j * 256, 256), 256)
                from_ = pl.ds(pl.multiple_of(f * 1024 + j * 256, 256), 256)
                part = jnp.dot(Asc[here, :], Wt[:, from_], preferred_element_type=F32)
                if q == 0:
                    TO[f, :, cols] = part
                else:
                    TS[q - 1, f, here, cols] = part.astype(BF16)

            if q == 3:
                scatter(q, f, first, last)
        if q in (1, 2):
            scatter(q, slice(None), first, last)

    def scatter(q, f, first, last):
        for i in range(first, last):
            d, ab = FAR[i // 2], i % 2
            here = pl.ds(i * 32, 32)
            there = pl.ds((q - 1) * 32, 32)
            rs[q].append(send(TS.at[q - 1, f, here], RT.at[f, ab, d - 1, there], far(ab)(d)))

    def transpose_acts(blocks):
        for i in blocks:
            At[:, i * 128:(i + 1) * 128] = Ax[...].reshape(768, FP)[i * 128:(i + 1) * 128, :].T

    gather(1)
    forward(0)
    gather(2)
    cross(0)
    forward(1, 0, 4)
    cross(1, 0, 4)
    forward(1, 4, 6)
    gather(3)
    cross(1, 4, 6)
    act(0)
    forward(2)
    cross(2)
    cot_copy.wait_recv()
    cotf[1 - zh, remote, :] = cotr[remote, :].astype(F32)
    act(1, 0, 4)
    act(1, 4, 6)
    forward(3, 0, 4)
    cross(3, 0, 4)
    forward(3, 4, 6)
    cross(3, 4, 6)
    cross_back(0)
    backward(1)
    act(2)
    backward(2)
    transpose_acts((2, 3))
    act(3, 0, 4)
    backward(3, 0, 4)
    act(3, 4, 6)
    backward(3, 4, 6)
    pass_on(0)
    backward(0)

    def write_hidden():
        row = lax.broadcasted_iota(jnp.int32, (192, 192), 0)
        there = absolute_row(lax.broadcasted_iota(jnp.int32, (1, 192), 1), y, x)
        pick = (row == there).astype(F32).astype(BF16)
        hidden_out[...] = jnp.dot(pick, H[zh], preferred_element_type=F32).astype(BF16)

    def weight_grads(first, last):
        @pl.loop(first, last)
        def _(j):
            cols = pl.ds(pl.multiple_of(j * 256, 256), 256)
            part = jnp.dot(
                At[...], X[:, :, cols].reshape(768, 256), preferred_element_type=F32
            ).astype(BF16)
            GG[0:FA, cols] = part[0:FA]
            GG[FA:FW, cols] = part[2 * FA:2 * FA + FT]
            UG[0:FA, cols] = part[FA:2 * FA]
            UG[FA:FW, cols] = part[2 * FA + FT:FP]

    def near_scatter(r, arrived):
        for cp in arrived:
            cp.wait_recv()
        out = [[], []]
        there = slice(r * 32, r * 32 + 32)
        for ab in range(2):
            for f in range(2):
                for fb in range(8):
                    cols = slice(fb * 128, (fb + 1) * 128)
                    v = TO[f, ab * 96 + r * 32:ab * 96 + r * 32 + 32, cols]
                    for i in range(3):
                        v = v + RT[f, ab, i, there, cols].astype(F32)
                    for k in range(4):
                        seat = (k % 2) * 2 + k // 2
                        at = pl.ds(seat * 16 + f * 8 + fb, 8, stride=64)
                        scr2[r, ab, at, :] = v[8 * k:8 * k + 8]
            R1s[r, ab] = scr2[r, ab].astype(BF16).reshape(4, 128, 128)
            near_at = at_x if ab == 0 else at_y
            for d in FAR:
                out[ab].append(send(R1s.at[r, ab, d], R1r.at[r, ab, d - 1], near_at(d)))
        return out

    def column_scatter(r, r1):
        for ab in range(2):
            for cp in r1[ab]:
                cp.wait_recv()
            v = scr2[r, ab, 0:128, :]
            for i in range(3):
                v = v + R1r[r, ab, i].astype(F32)
            R2f[r, 2 * ab:2 * ab + 2] = v.reshape(2, 2, 32, 128)
            R2s[r, 2 * ab:2 * ab + 2] = v.astype(BF16).reshape(2, 2, 32, 128)
        out = []
        for d, p in enumerate(zs_to):
            to = lax.rem(z + d + 1, 8)
            out.append(send(R2s.at[r, lax.rem(to, 4), lax.div(to, 4)], R2r.at[r, d], p))
        return out

    def column_sum(r, r2):
        acc[r, zh] = R2f[r, zl, zh]
        acc[r, 1 - zh] = jnp.zeros((32, 128), F32)
        for d, cp in enumerate(r2):
            cp.wait_recv()
            half = lax.div(lax.rem(z + 7 - d, 8), 4)
            acc[r, half] = acc[r, half] + R2r[r, d].astype(F32)
        theirs = pl.ds(pl.multiple_of((1 - c) * 16, 16), 16)
        for h in range(2):
            R3s[r, h] = acc[r, h, theirs, :].astype(BF16)
            at = pl.ds(pl.multiple_of(r * 64 + (h * 2 + c) * 16, 16), 16)
            tscr[at, :] = acc[r, h, pl.ds(pl.multiple_of(c * 16, 16), 16), :]

    r1 = [near_scatter(r, rs[r + 1]) for r in range(3)]
    transpose_acts((0, 1, 4, 5))
    weight_grads(0, 2)
    r2 = [column_scatter(r, r1[r]) for r in range(3)]
    weight_grads(2, 6)
    for r in range(3):
        column_sum(r, r2[r])
    r3 = send(R3s, R3r, sib)
    weight_grads(6, 8)
    write_hidden()
    r3.wait_recv()
    for r in range(3):
        for h in range(2):
            at = pl.ds(pl.multiple_of(r * 64 + (h * 2 + 1 - c) * 16, 16), 16)
            tscr[at, :] = R3r[r, h].astype(F32)
    for j in range(64):
        token_out[:, j * 128:(j + 1) * 128] = tscr[pl.ds(j, 3, stride=64), :].astype(BF16)

    for cp in copies:
        cp.wait_send()


def finish(*refs):
    n = len(refs) // 2
    sem = refs[-1]
    copies = [pltpu.make_async_copy(refs[i], refs[n + i], sem.at[i]) for i in range(n)]
    for cp in copies:
        cp.start()
    for cp in copies:
        cp.wait()


def on_device(tokens, gate_master, up_master, hidden_cotangent):
    vmem = pl.BlockSpec(memory_space=pltpu.VMEM)
    anywhere = pl.BlockSpec(memory_space=pl.ANY)
    V = pltpu.VMEM
    n_copies = 144
    shapes = ((192, FW), (3, 8192), (FW, DQ), (FW, DQ))
    results = pl.pallas_call(
        kernel,
        out_shape=tuple(V(shape, BF16) for shape in shapes),
        in_specs=[anywhere] * 4,
        out_specs=(vmem,) * 4,
        scratch_shapes=[
            V((3, 8192), BF16),
            V((192, FW), BF16),
            V((2, 4, 2, 2, 2, 3, 16, 128), BF16),
            V((2, 2, 3, 16, 128), BF16),
            V((2, 2, 3, 16, 128), BF16),
            V((2, 1536, 128), F32),
            V((4, 192, DQ), BF16),
            V((FP, DQ), BF16),
            V((FW, DQ), BF16),
            V((FW, DQ), BF16),
            V((5, 16, 128), F32),
            V((14, 16, 128), F32),
            V((192, FW), BF16),
            V((192, FW), BF16),
            V((2, 192, FW), F32),
            V((4, 2, 2, 48, FP), F32),
            V((4, 2, 48, FP), BF16),
            V((4, 2, 48, FP), BF16),
            V((48, FP), BF16),
            V((48, FP), BF16),
            V((3, 13, 48, 128), BF16),
            V((3, 13, 48, 128), BF16),
            V((4, 2, 2, 48, FP), BF16),
            V((4, 192, FP), BF16),
            V((192, FP), BF16),
            V((2, 192, FW), BF16),
            V((3, 2, 192, 1024), BF16),
            V((2, 192, 1024), F32),
            V((2, 2, 3, 96, 1024), BF16),
            V((3, 2, 512, 128), F32),
            V((3, 2, 4, 128, 128), BF16),
            V((3, 2, 3, 128, 128), BF16),
            V((3, 4, 2, 32, 128), F32),
            V((3, 4, 2, 32, 128), BF16),
            V((3, 7, 32, 128), BF16),
            V((3, 2, 32, 128), F32),
            V((3, 2, 16, 128), BF16),
            V((3, 2, 16, 128), BF16),
            V((192, 128), F32),
            V((FP, 768), BF16),
            pltpu.SemaphoreType.DMA((4, 2)),
            pltpu.SemaphoreType.DMA((2,)),
            pltpu.SemaphoreType.DMA((n_copies,)),
            pltpu.SemaphoreType.DMA((n_copies,)),
        ],
        compiler_params=pltpu.CompilerParams(
            collective_id=0, has_side_effects=True, vmem_limit_bytes=36 * 2**20
        ),
        name="swiglu_step",
    )(
        *(
            pltpu.with_memory_space_constraint(a, pltpu.HBM)
            for a in (tokens, gate_master.T, up_master.T, hidden_cotangent)
        )
    )
    hidden, token_grad, gate_grad, up_grad = pl.pallas_call(
        finish,
        out_shape=tuple(jax.ShapeDtypeStruct(shape, BF16) for shape in shapes),
        in_specs=[vmem] * 4,
        out_specs=(anywhere,) * 4,
        scratch_shapes=[pltpu.SemaphoreType.DMA((4,))],
        compiler_params=pltpu.CompilerParams(vmem_limit_bytes=8 * 2**20),
        name="finish",
    )(*(pltpu.with_memory_space_constraint(r, pltpu.VMEM) for r in results))
    return hidden, token_grad, gate_grad.T, up_grad.T


def solution(mesh):
    placed = (
        P(("group", "fsdp"), None),
        P("group", "fsdp"),
        P("group", "fsdp"),
        P("group", "fsdp"),
    )
    return jax.shard_map(
        on_device,
        mesh=mesh,
        in_specs=placed,
        out_specs=(
            P("group", "fsdp"),
            P(("group", "fsdp"), None),
            P("group", "fsdp"),
            P("group", "fsdp"),
        ),
        check_vma=False,
    )
```

```python
import functools

import jax
import jax.numpy as jnp
from jax import lax
from jax.experimental import pallas as pl
from jax.experimental.pallas import tpu as pltpu
from jax.sharding import PartitionSpec as P

QMAX = 60.0
EPS = 1e-06
MESH = pl.DeviceIdType.MESH
F32 = jnp.float32
BF16 = jnp.bfloat16

DQ = 2048
FW = 416
FA = 384
FT = FW - FA
FP = 2 * FW
SEAT = tuple((k % 2) * 6 + (k // 2 % 2) * 3 + k // 4 for k in range(12))
LOADS = ((0, 112), (112, 112), (224, 96), (320, 96))
FAR = (1, 3, 2)


def position():
    g = lax.axis_index("group")
    f = lax.axis_index("fsdp")
    return lax.div(g, 2), lax.rem(g, 2), lax.div(f, 16), lax.rem(lax.div(f, 4), 4), lax.rem(f, 4)


def place(zh, c, y, zl, x):
    return {"group": zh * 2 + c, "fsdp": y * 16 + zl * 4 + x}


def absolute_row(n, y, x):
    chunk, i, u = lax.div(n, 48), lax.div(lax.rem(n, 48), 8), lax.rem(n, 8)
    own = chunk == 0
    ab = jnp.where(own, lax.div(i, 3), lax.rem(i, 2))
    three = jnp.where(own, lax.rem(i, 3), lax.div(i, 2))
    near, zls = lax.div(u, 2), lax.rem(u, 2)
    d = jnp.where(own, 0, jnp.where(three == 0, FAR[0], jnp.where(three == 1, FAR[1], FAR[2])))
    r = jnp.where(own, three, chunk - 1)
    row_a = lax.rem(y + d, 4) * 16 + zls * 4 + lax.rem(x + near, 4)
    row_b = lax.rem(y + near, 4) * 16 + (zls + 2) * 4 + lax.rem(x + d, 4)
    return jnp.where(ab == 0, row_a, row_b) * 3 + r


def kernel(
    tokens_hbm, gate_hbm, up_hbm, cot_hbm,
    hidden_out, token_out, GG, UG,
    tokens, cot, S, tokb, TK, scr, X, Wt, gm, um, am_tx, am_rx, cotp, cotr, cotf,
    Pf, Ps, Pr, Q0s, Q0r, Qs, Qr, Ag, Ax, Asc, H, TS, TO, RT, scr2, R1s, R1r, R2f, R2s, R2r, acc, R3s, R3r, tscr,
    At,
    load_sem, in_sem, tx, rx,
):
    zh, c, y, zl, x = position()
    sib = place(zh, 1 - c, y, zl, x)
    anti = place(1 - zh, c, y, zl, x)
    z = zh * 4 + zl

    def at_x(d):
        return place(zh, c, y, zl, lax.rem(x + d, 4))

    def at_y(d):
        return place(zh, c, lax.rem(y + d, 4), zl, x)

    def at_z(d):
        to = lax.rem(z + d, 8)
        return place(lax.div(to, 4), c, y, lax.rem(to, 4), x)

    xs_to, ys_to = [at_x(d) for d in (1, 2, 3)], [at_y(d) for d in (1, 2, 3)]
    zs_to = [at_z(d) for d in range(1, 8)]

    used = [0]
    copies = []

    def send(src, dst, to):
        i = used[0]
        used[0] += 1
        cp = pltpu.make_async_remote_copy(
            src_ref=src, dst_ref=dst, send_sem=tx.at[i], recv_sem=rx.at[i],
            device_id=to, device_id_type=MESH,
        )
        cp.start()
        copies.append(cp)
        return cp

    small = []
    for i, (src, dst) in enumerate(((tokens_hbm, tokens), (cot_hbm, cot))):
        small.append(pltpu.make_async_copy(src, dst, in_sem.at[i]))
        small[i].start()
    loads = []
    for i, (start, count) in enumerate(LOADS):
        rows = pl.ds(start, count)
        for k, (src, dst) in enumerate(((gate_hbm, gm), (up_hbm, um))):
            cp = pltpu.make_async_copy(src.at[rows], dst.at[rows], load_sem.at[i, k])
            cp.start()
            loads.append(cp)
    barrier = pltpu.get_barrier_semaphore()
    peers = [sib] + xs_to + ys_to + zs_to
    for p in peers:
        pl.semaphore_signal(barrier, inc=1, device_id=p, device_id_type=MESH)

    small[0].wait()
    for j in range(64):
        tscr[pl.ds(j, 3, stride=64), :] = tokens[:, j * 128:(j + 1) * 128].astype(F32)
    for g in range(4):
        for r in range(3):
            tokb[g % 2, g // 2, r] = tscr[pl.ds(r * 64 + g * 16, 16), :].astype(BF16)

    tops = [jnp.zeros((16, DQ), BF16), jnp.zeros((16, DQ), BF16)]
    for i, (start, count) in enumerate(LOADS):
        for k, ref in enumerate((gm, um)):
            loads[2 * i + k].wait()

            def largest(b, top, ref=ref, start=start):
                rows = pl.ds(pl.multiple_of(start + b * 16, 16), 16)
                return jnp.maximum(top, jnp.abs(ref[rows, :]))

            tops[k] = lax.fori_loop(0, count // 16, largest, tops[k])
    for k in range(2):
        am_tx[0, pl.ds(8 * k, 8), :] = jnp.broadcast_to(
            jnp.max(tops[k].astype(F32), axis=(0, 1), keepdims=True), (8, 128)
        )

    pl.semaphore_wait(barrier, len(peers))

    t0 = send(tokb.at[1 - c], TK.at[:, c], sib)
    TK[:, c] = tokb[c]

    def share(stage, first, to):
        return [send(am_tx.at[stage], am_rx.at[first + i], p) for i, p in enumerate(to)]

    def merge(stage, first, cps):
        v = am_tx[stage]
        for i, cp in enumerate(cps):
            cp.wait_recv()
            v = jnp.maximum(v, am_rx[first + i])
        am_tx[stage + 1] = v

    m = share(0, 0, [sib])
    t0.wait_recv()
    near = S.at[lax.div(zl, 2), 0, lax.rem(zl, 2), zh]
    t1 = []
    for d, p in enumerate(zs_to):
        t1.append(send(TK.at[lax.div(lax.rem(z + d + 1, 8), 4)], near, p))
    near[...] = TK[zh]
    merge(0, 0, m)
    m = share(1, 1, xs_to)

    small[1].wait()
    mine = absolute_row(lax.broadcasted_iota(jnp.int32, (192, 1), 0), y, x)
    col = lax.broadcasted_iota(jnp.int32, (192, 192), 1)
    pick = (col == mine).astype(F32).astype(BF16)
    cperm = jnp.dot(pick, cot[...], preferred_element_type=F32)
    cotf[zh] = cperm
    cotp[...] = cperm.astype(BF16)
    merge(1, 1, m)
    m = share(2, 4, ys_to)
    merge(2, 4, m)
    m = share(3, 7, zs_to)
    for cp in t1:
        cp.wait_recv()
    s2 = [[], []]
    for d in (1, 3, 2):
        s2[0].append(send(S.at[0, 0], S.at[0, d], at_x(4 - d)))
        s2[1].append(send(S.at[1, 0], S.at[1, d], at_y(4 - d)))
    merge(3, 7, m)
    remote = pl.ds(48, 144)
    cot_copy = send(cotp.at[remote], cotr.at[remote], anti)

    g_amax = jnp.max(am_tx[4, 0:8, :], axis=(0, 1), keepdims=True)
    u_amax = jnp.max(am_tx[4, 8:16, :], axis=(0, 1), keepdims=True)
    g_factor, u_factor = QMAX / (g_amax + EPS), QMAX / (u_amax + EPS)
    g_scale, u_scale = (g_amax + EPS) / QMAX, (u_amax + EPS) / QMAX

    def quantized(ref, rows, factor):
        return jnp.floor(ref[rows, :].astype(F32) * factor + 0.5).astype(BF16)

    @pl.loop(0, FA // 16)
    def _(b):
        rows = pl.ds(pl.multiple_of(b * 16, 16), 16)
        Wt[rows, :] = quantized(gm, rows, g_factor)
        Wt[pl.ds(pl.multiple_of(FA + b * 16, 16), 16), :] = quantized(um, rows, u_factor)

    for t in range(0, FT, 16):
        Wt[2 * FA + t:2 * FA + t + 16, :] = quantized(gm, pl.ds(FA + t, 16), g_factor)
        Wt[2 * FA + FT + t:2 * FA + FT + t + 16, :] = quantized(um, pl.ds(FA + t, 16), u_factor)

    def far(ab):
        return at_y if ab == 0 else at_x

    for ab in range(2):
        for cp in s2[ab]:
            cp.wait_recv()
        scr[ab] = S[ab].reshape(1536, 128).astype(F32)
        for k in range(0, 12, 2):
            for fb in range(16):
                lo = scr[ab, pl.ds(SEAT[k] * 16 + fb, 8, stride=192), :]
                hi = scr[ab, pl.ds(SEAT[k + 1] * 16 + fb, 8, stride=192), :]
                at = ab * 96 + 8 * k
                X[0, at:at + 16, fb * 128:(fb + 1) * 128] = jnp.concatenate([lo, hi], axis=0).astype(BF16)

    big = {}

    def gather(q):
        big[q] = []
        for t, d in enumerate(FAR):
            for ab in range(2):
                own = pl.ds(ab * 96 + (q - 1) * 32, 32)
                there = pl.ds((t * 2 + ab) * 32, 32)
                big[q].append(send(X.at[0, own], X.at[q, there], far(ab)(4 - d)))

    p_copies, q_copies, sib_copies, anti_copies, fwd_copies = {}, {}, {}, {}, {}

    def forward(q, first=0, last=6):
        if q > 0:
            for cp in big[q][first:last]:
                cp.wait_recv()
        for n in range(0, FP, 256):
            width = min(256, FP - n)
            part = lax.dot_general(
                X[q, first * 32:last * 32, :], Wt[n:n + width, :],
                (((1,), (1,)), ((), ())), preferred_element_type=F32,
            )
            for i in range(first, last):
                for k in range(4):
                    at = ((i - first) * 4 + k) * 8
                    Pf[q, k // 2, k % 2, i * 8:i * 8 + 8, n:n + width] = part[at:at + 8]
        rows = pl.ds(first * 8, (last - first) * 8)
        Ps[q, :, rows, :] = Pf[q, 1 - c, :, rows, :].astype(BF16)
        p_copies[q, first] = send(Ps.at[q, :, rows], Pr.at[q, :, rows], sib)

    def cross(q, first=0, last=6):
        p_copies[q, first].wait_recv()
        rows = pl.ds(first * 8, (last - first) * 8)
        if q == 0:
            Q0s[...] = (Pf[q, c, 1 - zh] + Pr[q, 1 - zh].astype(F32)).astype(BF16)
            q_copies[q, first] = send(Q0s, Q0r, anti)
        else:
            tails = []
            for h in range(2):
                v = Pf[q, c, h, rows, :] + Pr[q, h, rows, :].astype(F32)
                for j in range(6):
                    Qs[q - 1, h * 6 + j, rows, :] = v[:, j * 128:(j + 1) * 128].astype(BF16)
                tails.append(v[:, 2 * FA:])
            Qs[q - 1, 12, rows, :] = jnp.concatenate(tails, axis=1).astype(BF16)
            q_copies[q, first] = send(Qs.at[q - 1, :, rows], Qr.at[q - 1, :, rows], anti)

    def act_rows(q, h, first, last):
        rows = pl.ds(first * 8, (last - first) * 8)
        pre = Pf[q, c, h, rows, :] + Pr[q, h, rows, :].astype(F32)
        if q == 0:
            pre = pre + Q0r[...].astype(F32)
        else:
            tail = Qr[q - 1, 12, rows, :].astype(F32)[:, h * 2 * FT:(h + 1) * 2 * FT]
            tiles = [Qr[q - 1, h * 6 + j, rows, :].astype(F32) for j in range(6)]
            pre = pre + jnp.concatenate(tiles + [tail], axis=1)
        gate = jnp.concatenate([pre[:, :FA], pre[:, 2 * FA:2 * FA + FT]], axis=1) * g_scale
        up = jnp.concatenate([pre[:, FA:2 * FA], pre[:, 2 * FA + FT:FP]], axis=1) * u_scale
        mine = pl.ds(q * 48 + first * 8, (last - first) * 8)
        cotangent = cotf[h, mine, :]
        sig = jax.nn.sigmoid(gate)
        silu = gate * sig
        H[h, mine, :] = (silu * up).astype(BF16)
        ga = cotangent * up * sig * (1.0 + gate * (1.0 - sig))
        ua = cotangent * silu
        packed = jnp.concatenate([ga[:, :FA], ua[:, :FA], ga[:, FA:], ua[:, FA:]], axis=1)
        Ag[q, c, h, rows, :] = packed.astype(BF16)

    def act(q, first=0, last=6):
        q_copies[q, first].wait_recv()
        if q == 0:
            act_rows(q, zh, first, last)
            mine = Ag.at[q, c, zh]
        else:
            for h in range(2):
                act_rows(q, h, first, last)
            mine = Ag.at[q, c, :, pl.ds(first * 8, (last - first) * 8)]
        sib_copies[q, first] = send(mine, mine, sib)

    def cross_back(q):
        anti_copies[q] = send(Ag.at[q, c, zh], Ag.at[q, c, zh], anti)

    def pass_on(q):
        anti_copies[q].wait_recv()
        fwd_copies[q] = send(Ag.at[q, c, 1 - zh], Ag.at[q, c, 1 - zh], sib)

    lane = lax.broadcasted_iota(jnp.int32, (1, FP), 1)
    is_gate = (lane < FA) | ((lane >= 2 * FA) & (lane < 2 * FA + FT))
    scale_row = jnp.where(is_gate, g_scale, u_scale)
    rs = {1: [], 2: [], 3: []}

    def backward(q, first=0, last=6):
        for f in range(first, last):
            if (q, f) in sib_copies:
                sib_copies[q, f].wait_recv()
        if q == 0:
            fwd_copies[q].wait_recv()
        mine = pl.ds(first * 8, (last - first) * 8)
        parts = [Ag[q, k // 2, k % 2, mine, :].astype(F32) for k in range(4)]
        rows = jnp.concatenate(
            [parts[k][i * 8:i * 8 + 8] for i in range(last - first) for k in range(4)], axis=0
        )
        here = pl.ds(first * 32, (last - first) * 32)
        Ax[q, here, :] = rows.astype(BF16)
        Asc[here, :] = (rows * scale_row).astype(BF16)
        for f in range(2):

            @pl.loop(0, 4)
            def _(j):
                cols = pl.ds(pl.multiple_of(j * 256, 256), 256)
                from_ = pl.ds(pl.multiple_of(f * 1024 + j * 256, 256), 256)
                part = jnp.dot(Asc[here, :], Wt[:, from_], preferred_element_type=F32)
                if q == 0:
                    TO[f, :, cols] = part
                else:
                    TS[q - 1, f, here, cols] = part.astype(BF16)

            if q == 3:
                scatter(q, f, first, last)
        if q in (1, 2):
            scatter(q, slice(None), first, last)

    def scatter(q, f, first, last):
        for i in range(first, last):
            d, ab = FAR[i // 2], i % 2
            here = pl.ds(i * 32, 32)
            there = pl.ds((q - 1) * 32, 32)
            rs[q].append(send(TS.at[q - 1, f, here], RT.at[f, ab, d - 1, there], far(ab)(d)))

    def transpose_acts(blocks):
        for i in blocks:
            At[:, i * 128:(i + 1) * 128] = Ax[...].reshape(768, FP)[i * 128:(i + 1) * 128, :].T

    gather(1)
    forward(0)
    gather(2)
    cross(0)
    forward(1, 0, 4)
    cross(1, 0, 4)
    forward(1, 4, 6)
    gather(3)
    cross(1, 4, 6)
    act(0)
    forward(2)
    cross(2)
    cot_copy.wait_recv()
    cotf[1 - zh, remote, :] = cotr[remote, :].astype(F32)
    act(1, 0, 4)
    act(1, 4, 6)
    forward(3, 0, 4)
    backward(1)
    cross(3, 0, 4)
    forward(3, 4, 6)
    cross(3, 4, 6)
    cross_back(0)
    act(2)
    transpose_acts((2,))
    backward(2)
    transpose_acts((3,))
    act(3, 0, 4)
    backward(3, 0, 4)
    act(3, 4, 6)
    backward(3, 4, 6)
    pass_on(0)
    backward(0)

    def write_hidden():
        row = lax.broadcasted_iota(jnp.int32, (192, 192), 0)
        there = absolute_row(lax.broadcasted_iota(jnp.int32, (1, 192), 1), y, x)
        pick = (row == there).astype(F32).astype(BF16)
        hidden_out[...] = jnp.dot(pick, H[zh], preferred_element_type=F32).astype(BF16)

    def weight_grads(first, last):
        @pl.loop(first, last)
        def _(j):
            cols = pl.ds(pl.multiple_of(j * 256, 256), 256)
            part = jnp.dot(
                At[...], X[:, :, cols].reshape(768, 256), preferred_element_type=F32
            ).astype(BF16)
            GG[0:FA, cols] = part[0:FA]
            GG[FA:FW, cols] = part[2 * FA:2 * FA + FT]
            UG[0:FA, cols] = part[FA:2 * FA]
            UG[FA:FW, cols] = part[2 * FA + FT:FP]

    def near_scatter(r, arrived):
        for cp in arrived:
            cp.wait_recv()
        out = [[], []]
        there = slice(r * 32, r * 32 + 32)
        for ab in range(2):
            for f in range(2):
                for fb in range(8):
                    cols = slice(fb * 128, (fb + 1) * 128)
                    v = TO[f, ab * 96 + r * 32:ab * 96 + r * 32 + 32, cols]
                    for i in range(3):
                        v = v + RT[f, ab, i, there, cols].astype(F32)
                    for k in range(4):
                        seat = (k % 2) * 2 + k // 2
                        at = pl.ds(seat * 16 + f * 8 + fb, 8, stride=64)
                        scr2[r, ab, at, :] = v[8 * k:8 * k + 8]
            R1s[r, ab] = scr2[r, ab].astype(BF16).reshape(4, 128, 128)
            near_at = at_x if ab == 0 else at_y
            for d in FAR:
                out[ab].append(send(R1s.at[r, ab, d], R1r.at[r, ab, d - 1], near_at(d)))
        return out

    def column_scatter(r, r1):
        for ab in range(2):
            for cp in r1[ab]:
                cp.wait_recv()
            v = scr2[r, ab, 0:128, :]
            for i in range(3):
                v = v + R1r[r, ab, i].astype(F32)
            R2f[r, 2 * ab:2 * ab + 2] = v.reshape(2, 2, 32, 128)
            R2s[r, 2 * ab:2 * ab + 2] = v.astype(BF16).reshape(2, 2, 32, 128)
        out = []
        for d, p in enumerate(zs_to):
            to = lax.rem(z + d + 1, 8)
            out.append(send(R2s.at[r, lax.rem(to, 4), lax.div(to, 4)], R2r.at[r, d], p))
        return out

    def column_sum(r, r2):
        acc[r, zh] = R2f[r, zl, zh]
        acc[r, 1 - zh] = jnp.zeros((32, 128), F32)
        for d, cp in enumerate(r2):
            cp.wait_recv()
            half = lax.div(lax.rem(z + 7 - d, 8), 4)
            acc[r, half] = acc[r, half] + R2r[r, d].astype(F32)
        theirs = pl.ds(pl.multiple_of((1 - c) * 16, 16), 16)
        for h in range(2):
            R3s[r, h] = acc[r, h, theirs, :].astype(BF16)
            at = pl.ds(pl.multiple_of(r * 64 + (h * 2 + c) * 16, 16), 16)
            tscr[at, :] = acc[r, h, pl.ds(pl.multiple_of(c * 16, 16), 16), :]

    r1 = [near_scatter(r, rs[r + 1]) for r in range(3)]
    transpose_acts((0, 1, 4, 5))
    weight_grads(0, 2)
    r2 = [column_scatter(r, r1[r]) for r in range(3)]
    weight_grads(2, 6)
    for r in range(3):
        column_sum(r, r2[r])
    r3 = send(R3s, R3r, sib)
    weight_grads(6, 8)
    write_hidden()
    r3.wait_recv()
    for r in range(3):
        for h in range(2):
            at = pl.ds(pl.multiple_of(r * 64 + (h * 2 + 1 - c) * 16, 16), 16)
            tscr[at, :] = R3r[r, h].astype(F32)
    for j in range(64):
        token_out[:, j * 128:(j + 1) * 128] = tscr[pl.ds(j, 3, stride=64), :].astype(BF16)

    for cp in copies:
        cp.wait_send()


def finish(*refs):
    n = len(refs) // 2
    sem = refs[-1]
    copies = [pltpu.make_async_copy(refs[i], refs[n + i], sem.at[i]) for i in range(n)]
    for cp in copies:
        cp.start()
    for cp in copies:
        cp.wait()


def on_device(tokens, gate_master, up_master, hidden_cotangent):
    vmem = pl.BlockSpec(memory_space=pltpu.VMEM)
    anywhere = pl.BlockSpec(memory_space=pl.ANY)
    V = pltpu.VMEM
    n_copies = 144
    shapes = ((192, FW), (3, 8192), (FW, DQ), (FW, DQ))
    results = pl.pallas_call(
        kernel,
        out_shape=tuple(V(shape, BF16) for shape in shapes),
        in_specs=[anywhere] * 4,
        out_specs=(vmem,) * 4,
        scratch_shapes=[
            V((3, 8192), BF16),
            V((192, FW), BF16),
            V((2, 4, 2, 2, 2, 3, 16, 128), BF16),
            V((2, 2, 3, 16, 128), BF16),
            V((2, 2, 3, 16, 128), BF16),
            V((2, 1536, 128), F32),
            V((4, 192, DQ), BF16),
            V((FP, DQ), BF16),
            V((FW, DQ), BF16),
            V((FW, DQ), BF16),
            V((5, 16, 128), F32),
            V((14, 16, 128), F32),
            V((192, FW), BF16),
            V((192, FW), BF16),
            V((2, 192, FW), F32),
            V((4, 2, 2, 48, FP), F32),
            V((4, 2, 48, FP), BF16),
            V((4, 2, 48, FP), BF16),
            V((48, FP), BF16),
            V((48, FP), BF16),
            V((3, 13, 48, 128), BF16),
            V((3, 13, 48, 128), BF16),
            V((4, 2, 2, 48, FP), BF16),
            V((4, 192, FP), BF16),
            V((192, FP), BF16),
            V((2, 192, FW), BF16),
            V((3, 2, 192, 1024), BF16),
            V((2, 192, 1024), F32),
            V((2, 2, 3, 96, 1024), BF16),
            V((3, 2, 512, 128), F32),
            V((3, 2, 4, 128, 128), BF16),
            V((3, 2, 3, 128, 128), BF16),
            V((3, 4, 2, 32, 128), F32),
            V((3, 4, 2, 32, 128), BF16),
            V((3, 7, 32, 128), BF16),
            V((3, 2, 32, 128), F32),
            V((3, 2, 16, 128), BF16),
            V((3, 2, 16, 128), BF16),
            V((192, 128), F32),
            V((FP, 768), BF16),
            pltpu.SemaphoreType.DMA((4, 2)),
            pltpu.SemaphoreType.DMA((2,)),
            pltpu.SemaphoreType.DMA((n_copies,)),
            pltpu.SemaphoreType.DMA((n_copies,)),
        ],
        compiler_params=pltpu.CompilerParams(
            collective_id=0, has_side_effects=True, vmem_limit_bytes=36 * 2**20
        ),
        name="swiglu_step",
    )(
        *(
            pltpu.with_memory_space_constraint(a, pltpu.HBM)
            for a in (tokens, gate_master.T, up_master.T, hidden_cotangent)
        )
    )
    hidden, token_grad, gate_grad, up_grad = pl.pallas_call(
        finish,
        out_shape=tuple(jax.ShapeDtypeStruct(shape, BF16) for shape in shapes),
        in_specs=[vmem] * 4,
        out_specs=(anywhere,) * 4,
        scratch_shapes=[pltpu.SemaphoreType.DMA((4,))],
        compiler_params=pltpu.CompilerParams(vmem_limit_bytes=8 * 2**20),
        name="finish",
    )(*(pltpu.with_memory_space_constraint(r, pltpu.VMEM) for r in results))
    return hidden, token_grad, gate_grad.T, up_grad.T


def solution(mesh):
    placed = (
        P(("group", "fsdp"), None),
        P("group", "fsdp"),
        P("group", "fsdp"),
        P("group", "fsdp"),
    )
    return jax.shard_map(
        on_device,
        mesh=mesh,
        in_specs=placed,
        out_specs=(
            P("group", "fsdp"),
            P(("group", "fsdp"), None),
            P("group", "fsdp"),
            P("group", "fsdp"),
        ),
        check_vma=False,
    )
```
